128 devices in a mesh: row: 8 (over z_hi, y), col: 4 (over z_lo, core), layer: 4 (over x).
Axes of the slice: x: 4, y: 4, z: 4 (z_hi: 2, z_lo: 2; z = z_hi * 2 + z_lo), core: 2. Of those that a mesh axis runs over, the one named last changes fastest.
Arguments:
- a_tiles: bfloat16 [8192, 12288], P('row', ('col', 'layer')), may hold values from -6 to 6
- a_occ: int32 [64, 96], P('row', ('col', 'layer')), may hold values from 0 to 1, as said below
- b_tiles: bfloat16 [4, 3072, 8192], P('layer', 'row', 'col'), may hold values from -0.09375 to 0.09375
- b_occ: int32 [4, 24, 64], P('layer', 'row', 'col'), may hold values from 0 to 1, as said below
Outputs:
- product: float32 [8192, 8192], P('row', ('col', 'layer'))
The draws below stay inside these ranges and needn't reach their ends.
Inputs may be any that keep to these rules, and one draw needn't show every extreme that they name: `a_occ`: 1 marks a tile of A that is present; a tile marked 0 is absent and its slot in a_tiles holds values that are not part of A. The 8 x 6 tiles of one device's block of A hold at most 24 present tiles, and some device's block holds exactly 24. `b_occ`: 1 marks a tile of B that is present; a tile marked 0 is absent and its slot in b_tiles holds values that are not part of B.
All inputs are finite; a program needn't handle non-finite values.
Results may differ from the reference program's by a relative error of at most 0.0003.
Values may be sent and summed in bfloat16 or wider, within the bound.
A program may use at most 128 MiB of HBM per device.

```python
import jax
import jax.numpy as jnp

TILE = 128
ROWT = 8
COLT = 16
GROUPT = 6
CAPS = 24
INNER_L = 24
MT = 64
NT = 64
KT = 96
N_COL = 4
N_LAYER = 4


def tile_pattern(key, row_count, col_count, row_group, col_group):
    subkeys = jax.random.split(key, 3)
    row_level = jax.random.randint(subkeys[0], (row_count // row_group,), 2, 9)
    col_level = jax.random.randint(subkeys[1], (col_count // col_group,), 2, 9)
    density = jnp.repeat(row_level, row_group)[:, None] * jnp.repeat(col_level, col_group)[None, :]
    rolled = jax.random.randint(subkeys[2], (row_count, col_count), 0, 64)
    return (rolled < density).astype(jnp.int32)


def draw_a_occ(key, part):
    key = jax.random.fold_in(key, 11)
    subkeys = jax.random.split(key, 3)
    row_blocks = MT // ROWT
    col_blocks = KT // GROUPT
    slot_count = ROWT * GROUPT
    block_count = row_blocks * col_blocks
    counts = jax.random.randint(subkeys[0], (block_count,), CAPS // 2, CAPS + 1)
    chosen = jax.random.randint(subkeys[1], (), 0, block_count)
    counts = jnp.where(jnp.arange(block_count) == chosen, CAPS, counts)
    scores = jax.random.randint(subkeys[2], (block_count, slot_count), 0, 1 << 20) * slot_count + jnp.arange(slot_count)[None, :]
    ranking = jnp.argsort(jnp.argsort(scores, axis=1), axis=1)
    present = (ranking < counts[:, None]).astype(jnp.int32)
    present = present.reshape(row_blocks, col_blocks, ROWT, GROUPT).transpose(0, 2, 1, 3)
    return present.reshape(MT, KT)


def draw_b_occ(key, part):
    key = jax.random.fold_in(key, 23)
    pattern = tile_pattern(key, N_LAYER * INNER_L, NT, GROUPT, COLT)
    return pattern.reshape(N_LAYER, INNER_L, NT)


def block_scale(key, extent, cuts, smallest, top_value):
    gain = 1.0
    for axis_at, shards_of in cuts:
        draws = jax.random.uniform(jax.random.fold_in(jax.random.fold_in(key, 6), axis_at), (shards_of,), jnp.float32, smallest / len(cuts), top_value / len(cuts))
        gain = gain * jnp.repeat(jnp.exp(draws), extent[axis_at] // shards_of).reshape((-1,) + (1,) * (len(extent) - 1 - axis_at))
    return gain


def noise(key, extent, scale, reach, cuts=(), kind=jnp.bfloat16):
    array = scale * jax.random.normal(key, extent, jnp.float32)
    if cuts:
        array = array * block_scale(key, extent, cuts, -0.22, 0.18)
    return jnp.clip(array, -reach, reach).astype(kind)


def setup_inputs(seed: int = 0) -> dict:
    streams_of = jax.random.split(jax.random.key(seed), 5)
    return {
        "a_tiles": noise(streams_of[0], (MT * TILE, KT * TILE), 1.0, 6.0, ((0, 8), (1, 16))),
        "a_occ": draw_a_occ(jax.random.fold_in(streams_of[4], 71), 0),
        "b_tiles": noise(streams_of[2], (N_LAYER, INNER_L * TILE, NT * TILE), (KT * TILE // 3) ** -0.5, 0.09375, ((0, 4), (1, 8), (2, 4))),
        "b_occ": draw_b_occ(jax.random.fold_in(streams_of[4], 71), 0),
    }


def zero_absent(tile_data, occupancy):
    full_shape = tile_data.shape
    leading = full_shape[:-2]
    row_count = full_shape[-2]
    col_count = full_shape[-1]
    tile_rows = occupancy.shape[-2]
    tile_cols = occupancy.shape[-1]
    tiled = tile_data.reshape(leading + (tile_rows, row_count // tile_rows, tile_cols, col_count // tile_cols))
    present = occupancy.astype(tile_data.dtype)[..., :, None, :, None]
    return (tiled * present).reshape(full_shape)


def reference(a_tiles, a_occ, b_tiles, b_occ):
    a_kept = zero_absent(a_tiles, a_occ)
    b_kept = zero_absent(b_tiles, b_occ)
    row_count = a_kept.shape[0]
    grouped = a_kept.reshape(row_count, N_COL, N_LAYER, GROUPT * TILE)
    running = jnp.zeros((row_count, b_kept.shape[2]), jnp.float32)
    for layer_index in range(N_LAYER):
        a_layer = grouped[:, :, layer_index, :].reshape(row_count, N_COL * GROUPT * TILE)
        running = running + jnp.dot(a_layer, b_kept[layer_index], preferred_element_type=jnp.float32)
    return running
```

```python
import jax
import jax.numpy as jnp
from jax import lax
from jax.experimental import pallas as pl
from jax.experimental.pallas import tpu as pltpu
from jax.sharding import PartitionSpec as P

MESH = pl.DeviceIdType.MESH
TILE = 128
ROWT = 8
GROUPT = 6
CAPS = 24
HALF = CAPS // 2
SLOTS = ROWT * GROUPT
BROWT = 3
COLT = 16
PIECE = BROWT * TILE
GROUP = GROUPT * TILE
ROWS = ROWT * TILE
NX = 4
NCOLS = COLT * TILE // NX
MIB = 1024 * 1024


def pack_kernel(a_occ, b_occ, a_ref, b_ref, packed, slots, kept):
    def place(t, used):
        i, j = t // GROUPT, lax.rem(t, GROUPT)
        row = pl.multiple_of(i * TILE, TILE)
        col = pl.multiple_of(j * TILE, TILE)
        packed[used] = a_ref[pl.ds(row, TILE), pl.ds(col, TILE)]
        here = a_occ[i, j]
        slots[t] = jnp.where(here != 0, used, CAPS)
        return used + jnp.where(here != 0, 1, 0)

    lax.fori_loop(0, SLOTS, place, jnp.int32(0))
    packed[CAPS] = jnp.zeros((TILE, TILE), jnp.bfloat16)
    for t in range(SLOTS, 128):
        slots[t] = CAPS
    for i in range(BROWT):
        for j in range(COLT):
            tile = b_ref[0, i * TILE : (i + 1) * TILE, j * TILE : (j + 1) * TILE]
            part, at = divmod(j, COLT // NX)
            present = b_occ[0, i, j] != 0
            kept[part, i * TILE : (i + 1) * TILE, at * TILE : (at + 1) * TILE] = jnp.where(
                present, tile, jnp.zeros_like(tile)
            )


def pack(a_tiles, a_occ, b_tiles, b_occ):
    vmem = pl.BlockSpec(memory_space=pltpu.VMEM)
    smem = pl.BlockSpec(memory_space=pltpu.SMEM)
    return pl.pallas_call(
        pack_kernel,
        out_shape=(
            jax.ShapeDtypeStruct((CAPS + 1, TILE, TILE), jnp.bfloat16),
            jax.ShapeDtypeStruct((128,), jnp.int32),
            jax.ShapeDtypeStruct((NX, PIECE, NCOLS), jnp.bfloat16),
        ),
        in_specs=[smem, smem, vmem, vmem],
        out_specs=(vmem, smem, vmem),
        compiler_params=pltpu.CompilerParams(vmem_limit_bytes=32 * MIB),
        name="pack",
    )(a_occ, b_occ, a_tiles, b_tiles)


A_KEYS = [(dx, dz, dc) for dx in range(4) for dz in range(2) for dc in range(2)]


def product_kernel(packed, slots, kept, out, *scratch):
    a_buf = dict(zip(A_KEYS, scratch[:16]))
    m_buf = dict(zip(A_KEYS, scratch[16:32]))
    b_buf, dense, send_sem, recv_sem, local_sem = scratch[32:]
    row, col, x = lax.axis_index("row"), lax.axis_index("col"), lax.axis_index("layer")
    zh, y, zl, c = row // 4, lax.rem(row, 4), col // 2, lax.rem(col, 2)

    def at_row(dz=0, dy=0):
        return lax.rem(zh + dz, 2) * 4 + lax.rem(y + dy + 4, 4)

    def at_col(dz=0, dc=0):
        return lax.rem(zl + dz, 2) * 2 + lax.rem(c + dc, 2)

    def at_layer(dx):
        return lax.rem(x + dx + 4, 4)

    def device(dx=0, dy=0, dzh=0, dzl=0, dc=0):
        return (at_row(dzh, dy), at_col(dzl, dc), at_layer(dx))

    neighbours = [
        dict(dx=1), dict(dx=-1), dict(dx=2), dict(dy=1), dict(dy=-1), dict(dzh=1), dict(dzl=1), dict(dc=1)
    ]
    barrier = pltpu.get_barrier_semaphore()
    for n in neighbours:
        pl.semaphore_signal(barrier, inc=1, device_id=device(**n), device_id_type=MESH)

    sends = []
    numbers = {}
    copies = {}

    def number(key):
        return numbers.setdefault(key, len(numbers))

    def send(key, src, dst, **to):
        n = number(key)
        copy = pltpu.make_async_remote_copy(
            src_ref=src, dst_ref=dst, send_sem=send_sem.at[n], recv_sem=recv_sem.at[n],
            device_id=device(**to), device_id_type=MESH,
        )
        copy.start()
        copies[key] = copy
        sends.append(copy)

    def wait(*keys):
        for key in keys:
            copies[key].wait_recv()

    def piece(dl, dz, dy, half=None):
        r = at_row(dz, dy)
        if half is None:
            return b_buf.at[at_layer(dl), pl.ds(pl.multiple_of(r * PIECE, PIECE), PIECE)]
        size = PIECE // 2
        start = pl.multiple_of(r * PIECE + half * size, size)
        return b_buf.at[at_layer(dl), pl.ds(start, size)]

    def tiles(key, half):
        return a_buf[key].at[pl.ds(half * HALF, HALF)]

    local = [
        pltpu.make_async_copy(packed, a_buf[0, 0, 0], local_sem.at[0]),
        pltpu.make_async_copy(slots, m_buf[0, 0, 0], local_sem.at[1]),
        pltpu.make_async_copy(kept.at[x], piece(0, 0, 0), local_sem.at[2]),
    ]
    for copy in local:
        copy.start()
    for key in A_KEYS[1:]:
        a_buf[key][CAPS] = jnp.zeros((TILE, TILE), jnp.bfloat16)
    pl.semaphore_wait(barrier, len(neighbours))

    def b_spread(d):
        send(("b", -d % 4, 0, 0), kept.at[at_layer(d)], b_buf.at[x, pl.ds(pl.multiple_of(row * PIECE, PIECE), PIECE)], dx=d)

    def b_y(dl, dz):
        src = kept.at[x] if (dl, dz) == (0, 0) else piece(dl, dz, 0)
        for d in (1, -1):
            send(("b", dl, dz, -d % 4), src, piece(dl, dz, 0), dy=d)

    def b_z(dl, dy):
        src = kept.at[x] if (dl, dy) == (0, 0) else piece(dl, 0, dy)
        send(("b", dl, 1, dy), src, piece(dl, 0, dy), dzh=1)

    def b_on(dl):
        send(("b", dl, 0, 2, 0), piece(dl, 0, -1, 0), piece(dl, 0, -1, 0), dy=1)
        send(("b", dl, 0, 2, 1), piece(dl, 0, 1, 1), piece(dl, 0, 1, 1), dy=-1)

    def a_z():
        send(("m", 0, 1, 0), slots, m_buf[0, 1, 0], dzl=1)
        for h in range(2):
            send(("a", 0, 1, 0, h), packed.at[pl.ds(h * HALF, HALF)], tiles((0, 1, 0), h), dzl=1)

    def a_x(dz):
        for d in (1, -1):
            key = (-d % 4, dz, 0)
            send(("m",) + key, slots if dz == 0 else m_buf[0, 1, 0], m_buf[key], dx=d)
        for h in range(2):
            src = packed.at[pl.ds(h * HALF, HALF)] if dz == 0 else tiles((0, 1, 0), h)
            for d in (1, -1):
                key = (-d % 4, dz, 0)
                hh = h if d == 1 else 1 - h
                src = packed.at[pl.ds(hh * HALF, HALF)] if dz == 0 else tiles((0, 1, 0), hh)
                send(("a",) + key + (hh,), src, tiles(key, hh), dx=d)

    def a_on(dz):
        send(("m", 2, dz, 0), m_buf[3, dz, 0], m_buf[2, dz, 0], dx=1)
        send(("a", 2, dz, 0, 0), tiles((3, dz, 0), 0), tiles((2, dz, 0), 0), dx=1)
        send(("a", 2, dz, 0, 1), tiles((1, dz, 0), 1), tiles((2, dz, 0), 1), dx=-1)

    def a_core(dx, dz):
        key, other = (dx, dz, 0), (dx, dz, 1)
        own = (dx, dz) == (0, 0)
        send(("m",) + other, slots if own else m_buf[key], m_buf[other], dc=1)
        send(("a",) + other, packed.at[pl.ds(0, CAPS)] if own else a_buf[key].at[pl.ds(0, CAPS)], a_buf[other].at[pl.ds(0, CAPS)], dc=1)

    def wait_a(dx, dz):
        wait(("m", dx, dz, 0), ("a", dx, dz, 0, 0), ("a", dx, dz, 0, 1))

    def wait_a_core(dx):
        for dz in range(2):
            wait(("m", dx, dz, 1), ("a", dx, dz, 1))

    def unpack(dx):
        for dz in range(2):
            for dc in range(2):
                key = (dx, dz, dc)
                group = at_col(dz, dc)

                def tile_row(i, carry, key=key, group=group):
                    at = pl.ds(pl.multiple_of(i * TILE, TILE), TILE)
                    for j in range(GROUPT):
                        slot = m_buf[key][i * GROUPT + j]
                        dense[group, at, j * TILE : (j + 1) * TILE] = a_buf[key][slot]
                    return carry

                lax.fori_loop(0, ROWT, tile_row, 0)

    first = [True]

    def multiply(dl, dz, dp):
        group = lax.rem(zh + dz, 2) * 2 + lax.rem(y // 2 + dp, 2)
        rows = pl.ds(pl.multiple_of(group * GROUP, GROUP), GROUP)
        start = first[0]
        first[0] = False

        def columns(n, carry):
            at = pl.ds(pl.multiple_of(n * 256, 256), 256)
            term = jnp.dot(dense[group], b_buf[at_layer(dl), rows, at], preferred_element_type=jnp.float32)
            if start:
                out[:, at] = term
            else:
                out[:, at] += term
            return carry

        lax.fori_loop(0, NCOLS // 256, columns, 0)

    b_y(0, 0)
    b_z(0, 0)
    for d in (1, 3, 2):
        b_spread(d)
    a_z()
    a_core(0, 0)
    a_x(0)
    for copy in local:
        copy.wait()

    wait(("b", 0, 1, 0))
    b_y(0, 1)
    for dl in (1, 3):
        wait(("b", dl, 0, 0))
        b_z(dl, 0)
    wait(("b", 0, 0, 1), ("b", 0, 0, 3))
    b_on(0)
    b_y(1, 0)
    b_y(3, 0)
    wait_a(0, 1)
    a_x(1)
    a_core(0, 1)
    wait(("b", 2, 0, 0))
    b_z(2, 0)
    wait_a_core(0)
    unpack(0)
    multiply(0, 0, 0)
    wait(("b", 0, 1, 1), ("b", 0, 1, 3))
    multiply(0, 1, 0)
    wait(("b", 0, 0, 2, 0), ("b", 0, 0, 2, 1))
    b_z(0, 2)
    multiply(0, 0, 1)

    for dl, after in ((1, 2), (3, None), (2, None)):
        wait(("b", dl, 1, 0))
        if dl != 2:
            b_y(dl, 1)
        wait(("b", dl, 0, 1), ("b", dl, 0, 3))
        b_on(dl)
        if dl == 2:
            b_y(dl, 1)
        if after is not None:
            b_y(after, 0)
        if dl == 1:
            wait(("b", 0, 1, 2))
            multiply(0, 1, 1)
            for dz in range(2):
                wait_a(1, dz)
                wait_a(3, dz)
                a_on(dz)
                a_core(1, dz)
                a_core(3, dz)
        if dl == 2:
            for dz in range(2):
                wait_a(2, dz)
                a_core(2, dz)
        wait_a_core(dl)
        unpack(dl)
        multiply(dl, 0, 0)
        wait(("b", dl, 0, 2, 0), ("b", dl, 0, 2, 1))
        b_z(dl, 2)
        multiply(dl, 0, 1)
        wait(("b", dl, 1, 1), ("b", dl, 1, 3))
        multiply(dl, 1, 0)
        wait(("b", dl, 1, 2))
        multiply(dl, 1, 1)

    for copy in sends:
        copy.wait_send()


N_COPIES = 3 + 4 * 8 + 14 + 8 + 15


def product(packed, slots, kept):
    anywhere = pl.BlockSpec(memory_space=pl.ANY)
    return pl.pallas_call(
        product_kernel,
        out_shape=jax.ShapeDtypeStruct((ROWS, NCOLS), jnp.float32),
        in_specs=[anywhere, anywhere, anywhere],
        out_specs=pl.BlockSpec(memory_space=pltpu.VMEM),
        scratch_shapes=[pltpu.VMEM((CAPS + 1, TILE, TILE), jnp.bfloat16)] * 16
        + [pltpu.SMEM((128,), jnp.int32)] * 16
        + [
            pltpu.VMEM((NX, 8 * PIECE, NCOLS), jnp.bfloat16),
            pltpu.VMEM((4, ROWS, GROUP), jnp.bfloat16),
            pltpu.SemaphoreType.DMA((N_COPIES,)),
            pltpu.SemaphoreType.DMA((N_COPIES,)),
            pltpu.SemaphoreType.DMA((3,)),
        ],
        compiler_params=pltpu.CompilerParams(
            collective_id=0, has_side_effects=True, vmem_limit_bytes=56 * MIB
        ),
        name="product",
    )(packed, slots, kept)


def shards(a_tiles, a_occ, b_tiles, b_occ):
    return product(*pack(a_tiles, a_occ, b_tiles, b_occ))


def solution(mesh):
    placed = (
        P("row", ("col", "layer")),
        P("row", ("col", "layer")),
        P("layer", "row", "col"),
        P("layer", "row", "col"),
    )
    return jax.shard_map(
        shards, mesh=mesh, in_specs=placed, out_specs=P("row", ("col", "layer")), check_vma=False
    )
```

```python
import jax
import jax.numpy as jnp
from jax import lax
from jax.experimental import pallas as pl
from jax.experimental.pallas import tpu as pltpu
from jax.sharding import PartitionSpec as P

MESH = pl.DeviceIdType.MESH
TILE = 128
ROWT = 8
GROUPT = 6
CAPS = 24
CUTS = 4
CUT = CAPS // CUTS
SLOTS = ROWT * GROUPT
BROWT = 3
COLT = 16
PIECE = BROWT * TILE
GROUP = GROUPT * TILE
ROWS = ROWT * TILE
NX = 4
NY = 4
NCOLS = COLT * TILE // NX
SIDES = 2
SIDE = NCOLS // SIDES
MIB = 1024 * 1024
OWN, OTHER = 0, 1
PARTS = 4
PART = ROWS // PARTS
LEVELS = 32767.0
SMALLEST = 1e-30

A_KEYS = [(dx, s, dc) for dx in range(4) for s in (OWN, OTHER) for dc in range(2)]
PLAN = [
    ("bs", 1, 1), ("bs", 1, 3), ("by", 1, 0), ("bs", 0, 1), ("bs", 0, 3), ("by", 0, 0), ("ax", "E", 0, 0),
    ("ax", "F", 1, 0), ("fq", 0), ("by", 1, 1), ("fq", 1), ("by", 0, 3), ("bs", 0, 2), ("by", 0, 1),
    ("ao", "F", 1, 0), ("ax", "E", 1, 0), ("fq", 2), ("ax", "E", 1, 2), ("ax", "E", 1, 1), ("bo", 0, 0),
    ("ax", "F", 1, 1), ("ax", "F", 1, 2), ("ac", 0, 0), ("ao", "E", 1, 0), ("ax", "F", 1, 3), ("by", 0, 2),
    ("bo", 0, 3), ("fq", 3), ("ax", "E", 1, 3), ("un", 0, 0), ("ac", 0, 1), ("ao", "F", 1, 1), ("ao", "F", 1, 2),
    ("by", 1, 3), ("ao", "E", 1, 1), ("ao", "E", 1, 2), ("ao", "E", 1, 3), ("ao", "F", 1, 3), ("bo", 0, 1),
    ("bs", 1, 2), ("ax", "E", 0, 3), ("ac", 1, 1), ("ax", "F", 0, 0), ("mu", 0, 0, 0), ("bo", 1, 1),
    ("ax", "F", 0, 2), ("ax", "E", 0, 2), ("un", 1, 1), ("ax", "E", 0, 1), ("bo", 1, 0), ("ax", "F", 0, 3),
    ("bo", 0, 2), ("ac", 3, 1), ("ax", "F", 0, 1), ("un", 0, 1), ("bo", 1, 3), ("un", 3, 1), ("mu", 1, 0, 0),
    ("ao", "E", 0, 0), ("ac", 2, 1), ("mu", 1, 3, 0), ("un", 2, 1), ("mu", 1, 1, 0), ("by", 1, 2), ("mu", 1, 2, 0),
    ("cs", 0), ("ao", "F", 0, 0), ("mu", 1, 0, 1), ("mu", 1, 3, 1), ("bo", 1, 2), ("ao", "E", 0, 2), ("mu", 1, 1, 1),
    ("mu", 1, 2, 1), ("ao", "F", 0, 2), ("cs", 1), ("ac", 3, 0), ("mu", 0, 0, 1), ("ao", "F", 0, 1), ("ac", 1, 0),
    ("ao", "E", 0, 1), ("ao", "E", 0, 3), ("ao", "F", 0, 3), ("cr", 0), ("un", 3, 0), ("un", 1, 0), ("mu", 0, 3, 0),
    ("mu", 0, 1, 1), ("mu", 0, 3, 1), ("ac", 2, 0), ("mu", 0, 1, 0), ("cr", 1), ("un", 2, 0), ("mu", 0, 2, 0),
    ("mu", 0, 2, 1),
]


def perform(op, env):
    kind = op[0]
    if kind == "bs":
        h, d = op[1:]
        env.send("EF", ("b", h, -d % 4, 0), dict(dx=d), lambda: env.spread(h, d))
    elif kind == "by":
        h, dl = op[1:]
        if dl:
            env.need("EF", ("b", h, dl, 0))
        for d in (1, -1):
            env.send("EF", ("b", h, dl, -d % 4), dict(dy=d), lambda: env.across(h, dl))
    elif kind == "bo":
        h, dl = op[1:]
        env.need("EF", ("b", h, dl, 3))
        env.send("EF", ("b", h, dl, 2, 0), dict(dy=1), lambda: env.onward(h, dl, -1, 0))
        env.need("EF", ("b", h, dl, 1))
        env.send("EF", ("b", h, dl, 2, 1), dict(dy=-1), lambda: env.onward(h, dl, 1, 1))
    elif kind == "az":
        for q in range(CUTS):
            env.send("E", ("a", 0, OWN, 0, q), dict(dzl=1), lambda q=q: env.start(OWN, q))
        for q in range(CUTS):
            env.send("F", ("a", 0, OTHER, 0, q), dict(dzh=1, dzl=1), lambda q=q: env.start(OTHER, q))
    elif kind == "fq":
        q = op[1]
        env.need("F", ("a", 0, OTHER, 0, q))
        env.send("F", ("a", 0, OTHER, 0, q), dict(dzl=1), lambda: env.block(0, OTHER, q, 0))
    elif kind == "ax":
        types, s, q = op[1:]
        env.need(types, ("a", 0, s, 0, q))
        for d in (1, -1):
            env.send(types, ("a", -d % 4, s, 0, q), dict(dx=d), lambda d=d: env.block(0, s, q, -d % 4))
    elif kind == "ao":
        types, s, q = op[1:]
        dx, d = (3, 1) if q < CUTS // 2 else (1, -1)
        env.need(types, ("a", dx, s, 0, q))
        env.send(types, ("a", 2, s, 0, q), dict(dx=d), lambda: env.block(dx, s, q, 2))
    elif kind == "av":
        types, s, q = op[1:]
        env.need(types, ("a", 2, s, 0, q))
        env.send(types, ("a", 2, s, 0, q), dict(dzl=1), lambda: env.block(2, s, q, 2))
    elif kind == "ac":
        dx, s = op[1:]
        for q in range(CUTS):
            env.need("EF", ("a", dx, s, 0, q))
        env.send("EF", ("a", dx, s, 1), dict(dc=1), lambda: env.twin(dx, s))
    elif kind == "un":
        dx, s = op[1:]
        for q in range(CUTS):
            env.need("EF", ("a", dx, s, 0, q))
        env.need("EF", ("a", dx, s, 1))
        env.compute("unpack", dx, s)
    elif kind == "mu":
        s, dl, h = op[1:]
        env.need("EF", ("b", h, dl, 0))
        env.need("EF", ("b", h, dl, 1), ("b", h, dl, 3), ("b", h, dl, 2, 0), ("b", h, dl, 2, 1))
        env.compute("multiply", s, dl, h)
    elif kind == "cs":
        h = op[1]
        env.compute("code", h)
        env.send("EF", ("s", h), dict(dzh=1), lambda: env.steps(h))
        for q in range(PARTS):
            env.send("EF", ("c", h, q), dict(dzh=1), lambda q=q: env.part(h, q))
    elif kind == "cr":
        h = op[1]
        env.need("EF", ("s", h))
        for q in range(PARTS):
            env.need("EF", ("c", h, q))
            env.compute("add", h, q)


def product_kernel(a_occ, b_occ, a_hbm, b_hbm, out, *scratch):
    a_buf = dict(zip(A_KEYS, scratch[:16]))
    m_buf = dict(zip(A_KEYS, scratch[16:32]))
    (a_in, a_cut, b_in, packed, slots, after, kept, b_buf, dense, partial, coded, coded_in, steps, steps_in, send_sem, recv_sem, local_sem) = scratch[32:]
    row, col, x = lax.axis_index("row"), lax.axis_index("col"), lax.axis_index("layer")
    zh, y, zl, c = row // 4, lax.rem(row, 4), col // 2, lax.rem(col, 2)
    even = zh == zl
    odd = jnp.logical_not(even)

    def at_layer(dx):
        return lax.rem(x + dx + 4, 4)

    def device(dx=0, dy=0, dzh=0, dzl=0, dc=0):
        return (
            lax.rem(zh + dzh, 2) * 4 + lax.rem(y + dy + 4, 4),
            lax.rem(zl + dzl, 2) * 2 + lax.rem(c + dc, 2),
            at_layer(dx),
        )

    get_b = pltpu.make_async_copy(b_hbm.at[0], b_in, local_sem.at[0])
    get_a = pltpu.make_async_copy(a_hbm, a_in, local_sem.at[1])
    get_b.start()
    get_a.start()
    neighbours = [
        dict(dx=1), dict(dx=-1), dict(dx=2), dict(dy=1), dict(dy=-1), dict(dzl=1), dict(dzh=1), dict(dzh=1, dzl=1), dict(dc=1)
    ]
    barrier = pltpu.get_barrier_semaphore()
    for n in neighbours:
        pl.semaphore_signal(barrier, inc=1, device_id=device(**n), device_id_type=MESH)

    numbers, places, used = {}, {}, [0]
    beside = device(dx=1)
    started = {"EF": [], "E": [], "F": []}
    waited = {"E": set(), "F": set()}
    begun = set()

    def when(types, fn):
        if types == "EF":
            fn()
        else:
            pl.when(even if types == "E" else odd)(fn)

    def remote(src, dst, n, m, to):
        return pltpu.make_async_remote_copy(
            src_ref=src, dst_ref=dst, send_sem=send_sem.at[m], recv_sem=recv_sem.at[n], device_id=to, device_id_type=MESH
        )

    def put(types, key, src, dst, to):
        n = numbers.setdefault(key, len(numbers))
        m = used[0]
        used[0] += 1
        remote(src, dst, n, m, device(**to)).start()
        places[key] = dst
        started[types].append((src, dst, n, m))

    def take(key):
        if key[0] == "own":
            own_copy().wait()
            return
        dst = places[key]
        remote(dst, dst, numbers[key], 0, beside).wait_recv()

    def piece(h, dl, dy, part=None):
        start = lax.rem(y + dy + 4, 4) * PIECE
        size = PIECE
        if part is not None:
            size = PIECE // 2
            start = start + part * size
        return b_buf.at[h, at_layer(dl), pl.ds(pl.multiple_of(start, size), size)]

    def tiles(ref, q):
        return ref.at[pl.ds(q * CUT, CUT)]

    def own_copy():
        return pltpu.make_async_copy(packed, a_buf[0, OWN, 0].at[pl.ds(0, CAPS)], local_sem.at[4])

    class Env:
        def need(self, types, *keys):
            late = {"EF": [], "E": [], "F": []}
            for key in keys:
                full = [key]
                if key[0] == "a" and (key[3] == 1 or key[4] == 0):
                    full = [("m",) + key[1:4], key]
                for name in full:
                    todo = {}
                    for t in types:
                        k = ("own",) if t == "E" and name[0] in "am" and name[1:4] == (0, OWN, 0) else name
                        if k[0] == "b" and k[2:] == (0, 0):
                            k = ("mine", k[1])
                        if k not in waited[t]:
                            waited[t].add(k)
                            todo[t] = k
                    if len(todo) == 2 and todo["E"] == todo["F"]:
                        late["EF"].append(todo["E"])
                    else:
                        for t, k in todo.items():
                            late[t].append(k)
            for t, ks in late.items():
                if ks:

                    def waits(ks=ks):
                        for k in ks:
                            if k[0] == "mine":
                                mine(k[1]).wait()
                            else:
                                take(k)

                    when(t, waits)

        def send(self, types, key, to, refs):
            def go():
                for name, src, dst in refs():
                    put(types, name or key, src, dst, to)

            when(types, go)

        def compute(self, what, *args):
            dict(unpack=unpack, multiply=multiply, code=code, add=add)[what](*args)

        def spread(self, h, d):
            return [(None, kept.at[at_layer(d), h], b_buf.at[h, x, pl.ds(pl.multiple_of(y * PIECE, PIECE), PIECE)])]

        def across(self, h, dl):
            return [(None, kept.at[x, h] if dl == 0 else piece(h, dl, 0), piece(h, dl, 0))]

        def onward(self, h, dl, dy, part):
            return [(None, piece(h, dl, dy, part), piece(h, dl, dy, part))]

        def start(self, s, q):
            slow = [(("m", 0, s, 0), slots, m_buf[0, s, 0])] if q == 0 else []
            return slow + [(None, tiles(packed, q), tiles(a_buf[0, s, 0], q))]

        def block(self, dx, s, q, to):
            slow = [(("m", to, s, 0), m_buf[dx, s, 0], m_buf[to, s, 0])] if q == 0 else []
            return slow + [(None, tiles(a_buf[dx, s, 0], q), tiles(a_buf[to, s, 0], q))]

        def twin(self, dx, s):
            here, there = pl.ds(0, CAPS), (dx, s, 1)
            return [
                (("m", dx, s, 1), m_buf[dx, s, 0], m_buf[there]),
                (None, a_buf[dx, s, 0].at[here], a_buf[there].at[here]),
            ]

        def steps(self, h):
            return [(None, steps.at[h], steps_in.at[h])]

        def part(self, h, q):
            rows = pl.ds(q * PART, PART)
            return [(None, coded.at[h, rows], coded_in.at[h, rows])]

    def mine(h):
        return pltpu.make_async_copy(kept.at[x, h], piece(h, 0, 0), local_sem.at[2 + h])

    def unpack(dx, s):
        for dc in range(2):
            key = (dx, s, dc)
            group = lax.rem(c + dc, 2)

            def tile_row(i, carry, key=key, group=group):
                at = pl.ds(pl.multiple_of(i * TILE, TILE), TILE)
                for j in range(GROUPT):
                    slot = m_buf[key][i * GROUPT + j]
                    dense[s, dx, group, at, j * TILE : (j + 1) * TILE] = a_buf[key][slot]
                return carry

            lax.fori_loop(0, ROWT, tile_row, 0)

    def multiply(s, dl, h):
        into = partial.at[h] if s == OTHER else out.at[:, pl.ds(h * SIDE, SIDE)]
        term = jnp.dot(dense[s, dl, 0], b_buf[h, at_layer(dl), :GROUP], preferred_element_type=jnp.float32)
        term += jnp.dot(dense[s, dl, 1], b_buf[h, at_layer(dl), GROUP:], preferred_element_type=jnp.float32)
        if (s, h) in begun:
            into[...] += term
        else:
            into[...] = term
        begun.add((s, h))

    def code(h):
        for q in range(PARTS):
            part = pl.ds(q * PART, PART)
            block = partial[h, part]
            most = jnp.max(jnp.abs(block), axis=0, keepdims=True)
            some = most > SMALLEST
            steps[h, q : q + 1] = jnp.where(some, most * (1.0 / LEVELS), 0.0)
            ups = jnp.where(some, LEVELS / jnp.where(some, most, 1.0), 0.0)
            coded[h, part] = jnp.round(block * ups).astype(jnp.int32).astype(jnp.int16)

    def add(h, q):
        part = pl.ds(q * PART, PART)
        out[part, pl.ds(h * SIDE, SIDE)] += coded_in[h, part].astype(jnp.float32) * steps_in[h, q : q + 1]

    def pack():
        def scan(i, nxt):
            t = SLOTS - 1 - i
            here = a_occ[t // GROUPT, lax.rem(t, GROUPT)] != 0
            nxt = jnp.where(here, t, nxt)
            after[t] = nxt
            return nxt

        after[SLOTS] = SLOTS - 1
        first = lax.fori_loop(0, SLOTS, scan, jnp.int32(SLOTS - 1))

        def name(t, used):
            here = a_occ[t // GROUPT, lax.rem(t, GROUPT)] != 0
            slots[t] = jnp.where(here, used, CAPS)
            return used + jnp.where(here, 1, 0)

        lax.fori_loop(0, SLOTS, name, jnp.int32(0))

        def place(s, t):
            packed[s] = a_cut[t]
            return after[t + 1]

        for t in range(SLOTS):
            i, j = divmod(t, GROUPT)
            a_cut[t] = a_in[i * TILE : (i + 1) * TILE, j * TILE : (j + 1) * TILE]

        lax.fori_loop(0, CAPS, place, first)

    for key in A_KEYS:
        a_buf[key][CAPS] = jnp.zeros((TILE, TILE), jnp.bfloat16)

    env = Env()
    get_a.wait()
    pack()
    pl.semaphore_wait(barrier, len(neighbours))
    perform(("az",), env)

    @pl.when(even)
    def _():
        own_copy().start()

        def keep_slot(t, carry):
            m_buf[0, OWN, 0][t] = slots[t]
            return carry

        lax.fori_loop(0, SLOTS, keep_slot, 0)

    get_b.wait()
    for part in range(NX):
        for i in range(BROWT):
            for k in range(COLT // NX):
                j = part * (COLT // NX) + k
                h, at = divmod(k, COLT // NX // SIDES)
                tile = b_in[i * TILE : (i + 1) * TILE, j * TILE : (j + 1) * TILE]
                present = b_occ[0, i, j] != 0
                kept[part, h, i * TILE : (i + 1) * TILE, at * TILE : (at + 1) * TILE] = jnp.where(
                    present, tile, jnp.zeros_like(tile)
                )
    for h in range(SIDES):
        mine(h).start()

    for op in PLAN:
        perform(op, env)

    for types, copies in started.items():

        def sent(copies=copies):
            for src, dst, n, m in copies:
                remote(src, dst, n, m, beside).wait_send()

        when(types, sent)


def shards(a_tiles, a_occ, b_tiles, b_occ):
    anywhere = pl.BlockSpec(memory_space=pl.ANY)
    smem = pl.BlockSpec(memory_space=pltpu.SMEM)
    return pl.pallas_call(
        product_kernel,
        out_shape=jax.ShapeDtypeStruct((ROWS, NCOLS), jnp.float32),
        in_specs=[smem, smem, anywhere, anywhere],
        out_specs=pl.BlockSpec(memory_space=pltpu.VMEM),
        scratch_shapes=[pltpu.VMEM((CAPS + 1, TILE, TILE), jnp.bfloat16)] * 16
        + [pltpu.SMEM((128,), jnp.int32)] * 16
        + [
            pltpu.VMEM((ROWS, GROUP), jnp.bfloat16),
            pltpu.VMEM((SLOTS, TILE, TILE), jnp.bfloat16),
            pltpu.VMEM((PIECE, NX * NCOLS), jnp.bfloat16),
            pltpu.VMEM((CAPS, TILE, TILE), jnp.bfloat16),
            pltpu.SMEM((128,), jnp.int32),
            pltpu.SMEM((128,), jnp.int32),
            pltpu.VMEM((NX, SIDES, PIECE, SIDE), jnp.bfloat16),
            pltpu.VMEM((SIDES, NX, NY * PIECE, SIDE), jnp.bfloat16),
            pltpu.VMEM((2, NX, 2, ROWS, GROUP), jnp.bfloat16),
            pltpu.VMEM((SIDES, ROWS, SIDE), jnp.float32),
            pltpu.VMEM((SIDES, ROWS, SIDE), jnp.int16),
            pltpu.VMEM((SIDES, ROWS, SIDE), jnp.int16),
            pltpu.VMEM((SIDES, 8, SIDE), jnp.float32),
            pltpu.VMEM((SIDES, 8, SIDE), jnp.float32),
            pltpu.SemaphoreType.DMA((200,)),
            pltpu.SemaphoreType.DMA((200,)),
            pltpu.SemaphoreType.DMA((5,)),
        ],
        compiler_params=pltpu.CompilerParams(
            collective_id=0, has_side_effects=True, vmem_limit_bytes=60 * MIB
        ),
        name="product",
    )(a_occ, b_occ, a_tiles, b_tiles)


def solution(mesh):
    placed = (
        P("row", ("col", "layer")),
        P("row", ("col", "layer")),
        P("layer", "row", "col"),
        P("layer", "row", "col"),
    )
    return jax.shard_map(
        shards, mesh=mesh, in_specs=placed, out_specs=P("row", ("col", "layer")), check_vma=False
    )
```

```python
import jax
import jax.numpy as jnp
from jax import lax
from jax.experimental import pallas as pl
from jax.experimental.pallas import tpu as pltpu
from jax.sharding import PartitionSpec as P

MESH = pl.DeviceIdType.MESH
TILE = 128
ROWT = 8
GROUPT = 6
CAPS = 24
CUTS = 4
CUT = CAPS // CUTS
SLOTS = ROWT * GROUPT
BROWT = 3
COLT = 16
PIECE = BROWT * TILE
GROUP = GROUPT * TILE
ROWS = ROWT * TILE
NX = 4
NY = 4
NCOLS = COLT * TILE // NX
SIDES = 2
SIDE = NCOLS // SIDES
MIB = 1024 * 1024
OWN, OTHER = 0, 1
PARTS = 4
PART = ROWS // PARTS
LEVELS = 32767.0
SMALLEST = 1e-30

A_KEYS = [(dx, s, dc) for dx in range(4) for s in (OWN, OTHER) for dc in range(2)]
PLAN = [
    ("bs", 1, 2), ("by", 0, 0), ("by", 1, 0), ("bs", 0, 1), ("bs", 0, 3), ("bs", 0, 2), ("by", 1, 2), ("fq", 1),
    ("bs", 1, 3), ("by", 0, 3), ("ax", "E", 0, 1), ("ax", "F", 1, 1), ("ax", "E", 1, 1), ("ax", "F", 1, 2),
    ("fq", 0), ("bo", 1, 0), ("ac", 0, 0), ("fq", 3), ("ax", "E", 1, 0), ("by", 0, 2), ("bo", 0, 0), ("fq", 2),
    ("un", 0, 0), ("ax", "F", 1, 3), ("by", 1, 1), ("ax", "E", 1, 3), ("ax", "E", 1, 2), ("ac", 0, 1),
    ("ax", "F", 1, 0), ("by", 0, 1), ("bo", 0, 3), ("mu", 0, 0, 1), ("mu", 0, 0, 0), ("ao", "F", 1, 1), ("bs", 1, 1),
    ("un", 0, 1), ("ao", "E", 1, 3), ("ao", "F", 1, 0), ("ao", "E", 1, 0), ("ac", 3, 1), ("ao", "F", 1, 2),
    ("ax", "E", 0, 3), ("bo", 0, 2), ("un", 3, 1), ("ao", "F", 1, 3), ("av", "F", 1, 1), ("bo", 0, 1), ("bo", 1, 1),
    ("ax", "F", 0, 2), ("ac", 1, 1), ("ax", "F", 0, 0), ("ax", "E", 0, 2), ("mu", 1, 0, 0), ("un", 1, 1),
    ("av", "F", 1, 2), ("ax", "E", 0, 0), ("ax", "F", 0, 1), ("by", 1, 3), ("mu", 1, 1, 0), ("bo", 1, 2),
    ("ao", "E", 0, 1), ("ac", 2, 1), ("mu", 1, 3, 0), ("un", 2, 1), ("mu", 1, 2, 0), ("cs", 0), ("bo", 1, 3),
    ("mu", 1, 1, 1), ("ax", "F", 0, 3), ("mu", 1, 2, 1), ("ao", "F", 0, 2), ("ao", "E", 0, 3), ("ao", "F", 0, 1),
    ("mu", 1, 0, 1), ("mu", 1, 3, 1), ("ac", 1, 0), ("ao", "F", 0, 3), ("ac", 3, 0), ("ao", "F", 0, 0),
    ("ao", "E", 0, 0), ("ao", "E", 0, 2), ("cs", 1), ("un", 1, 0), ("un", 3, 0), ("mu", 0, 1, 1), ("mu", 0, 3, 0),
    ("mu", 0, 3, 1), ("cr", 0), ("ac", 2, 0), ("mu", 0, 1, 0), ("un", 2, 0), ("mu", 0, 2, 1), ("mu", 0, 2, 0),
    ("cr", 1),
]


def perform(op, env):
    kind = op[0]
    if kind == "bs":
        h, d = op[1:]
        env.send("EF", ("b", h, -d % 4, 0), dict(dx=d), lambda: env.spread(h, d))
    elif kind == "by":
        h, dl = op[1:]
        if dl:
            env.need("EF", ("b", h, dl, 0))
        for d in (1, -1):
            env.send("EF", ("b", h, dl, -d % 4), dict(dy=d), lambda: env.across(h, dl))
    elif kind == "bo":
        h, dl = op[1:]
        env.need("EF", ("b", h, dl, 3))
        env.send("EF", ("b", h, dl, 2, 0), dict(dy=1), lambda: env.onward(h, dl, -1, 0))
        env.need("EF", ("b", h, dl, 1))
        env.send("EF", ("b", h, dl, 2, 1), dict(dy=-1), lambda: env.onward(h, dl, 1, 1))
    elif kind == "az":
        for q in range(CUTS):
            env.send("E", ("a", 0, OWN, 0, q), dict(dzl=1), lambda q=q: env.start(OWN, q))
        for q in range(CUTS):
            env.send("F", ("a", 0, OTHER, 0, q), dict(dzh=1, dzl=1), lambda q=q: env.start(OTHER, q))
    elif kind == "fq":
        q = op[1]
        env.need("F", ("a", 0, OTHER, 0, q))
        env.send("F", ("a", 0, OTHER, 0, q), dict(dzl=1), lambda: env.block(0, OTHER, q, 0))
    elif kind == "ax":
        types, s, q = op[1:]
        env.need(types, ("a", 0, s, 0, q))
        for d in (1, -1):
            env.send(types, ("a", -d % 4, s, 0, q), dict(dx=d), lambda d=d: env.block(0, s, q, -d % 4))
    elif kind == "ao":
        types, s, q = op[1:]
        dx, d = (3, 1) if q < CUTS // 2 else (1, -1)
        env.need(types, ("a", dx, s, 0, q))
        env.send(types, ("a", 2, s, 0, q), dict(dx=d), lambda: env.block(dx, s, q, 2))
    elif kind == "av":
        types, s, q = op[1:]
        env.need(types, ("a", 2, s, 0, q))
        env.send(types, ("a", 2, s, 0, q), dict(dzl=1), lambda: env.block(2, s, q, 2))
    elif kind == "ac":
        dx, s = op[1:]
        for q in range(CUTS):
            env.need("EF", ("a", dx, s, 0, q))
        env.send("EF", ("a", dx, s, 1), dict(dc=1), lambda: env.twin(dx, s))
    elif kind == "un":
        dx, s = op[1:]
        for q in range(CUTS):
            env.need("EF", ("a", dx, s, 0, q))
        env.need("EF", ("a", dx, s, 1))
        env.compute("unpack", dx, s)
    elif kind == "mu":
        s, dl, h = op[1:]
        env.need("EF", ("b", h, dl, 0))
        env.need("EF", ("b", h, dl, 1), ("b", h, dl, 3), ("b", h, dl, 2, 0), ("b", h, dl, 2, 1))
        env.compute("multiply", s, dl, h)
    elif kind == "cs":
        h = op[1]
        env.compute("code", h)
        env.send("EF", ("s", h), dict(dzh=1), lambda: env.steps(h))
        for q in range(PARTS):
            env.send("EF", ("c", h, q), dict(dzh=1), lambda q=q: env.part(h, q))
    elif kind == "cr":
        h = op[1]
        env.need("EF", ("s", h))
        for q in range(PARTS):
            env.need("EF", ("c", h, q))


def product_kernel(a_occ, b_occ, a_hbm, b_hbm, out, coded_in, steps_in, *scratch):
    a_buf = dict(zip(A_KEYS, scratch[:16]))
    m_buf = dict(zip(A_KEYS, scratch[16:32]))
    (a_in, a_cut, b_in, packed, slots, after, kept, b_buf, dense, partial, coded, steps, send_sem, recv_sem, local_sem) = scratch[32:]
    row, col, x = lax.axis_index("row"), lax.axis_index("col"), lax.axis_index("layer")
    zh, y, zl, c = row // 4, lax.rem(row, 4), col // 2, lax.rem(col, 2)
    even = zh == zl
    odd = jnp.logical_not(even)

    def at_layer(dx):
        return lax.rem(x + dx + 4, 4)

    def device(dx=0, dy=0, dzh=0, dzl=0, dc=0):
        return (
            lax.rem(zh + dzh, 2) * 4 + lax.rem(y + dy + 4, 4),
            lax.rem(zl + dzl, 2) * 2 + lax.rem(c + dc, 2),
            at_layer(dx),
        )

    get_b = pltpu.make_async_copy(b_hbm.at[0], b_in, local_sem.at[0])
    get_a = pltpu.make_async_copy(a_hbm, a_in, local_sem.at[1])
    get_b.start()
    get_a.start()
    neighbours = [
        dict(dx=1), dict(dx=-1), dict(dx=2), dict(dy=1), dict(dy=-1), dict(dzl=1), dict(dzh=1), dict(dzh=1, dzl=1), dict(dc=1)
    ]
    barrier = pltpu.get_barrier_semaphore()
    for n in neighbours:
        pl.semaphore_signal(barrier, inc=1, device_id=device(**n), device_id_type=MESH)

    numbers, places, used = {}, {}, [0]
    beside = device(dx=1)
    started = {"EF": [], "E": [], "F": []}
    waited = {"E": set(), "F": set()}
    begun = set()

    def when(types, fn):
        if types == "EF":
            fn()
        else:
            pl.when(even if types == "E" else odd)(fn)

    def remote(src, dst, n, m, to):
        return pltpu.make_async_remote_copy(
            src_ref=src, dst_ref=dst, send_sem=send_sem.at[m], recv_sem=recv_sem.at[n], device_id=to, device_id_type=MESH
        )

    def put(types, key, src, dst, to):
        n = numbers.setdefault(key, len(numbers))
        m = used[0]
        used[0] += 1
        remote(src, dst, n, m, device(**to)).start()
        places[key] = dst
        started[types].append((src, dst, n, m))

    def take(key):
        if key[0] == "own":
            own_copy().wait()
            return
        n = numbers.setdefault(key, len(numbers))
        if key[0] == "a":
            dst = tiles(a_buf[key[1:4]], key[4]) if len(key) == 5 else a_buf[key[1:4]].at[pl.ds(0, CAPS)]
        elif key[0] == "m":
            dst = m_buf[key[1:4]]
        else:
            dst = places[key]
        remote(dst, dst, n, 0, beside).wait_recv()

    def piece(h, dl, dy, part=None):
        start = lax.rem(y + dy + 4, 4) * PIECE
        size = PIECE
        if part is not None:
            size = PIECE // 2
            start = start + part * size
        return b_buf.at[h, at_layer(dl), pl.ds(pl.multiple_of(start, size), size)]

    def tiles(ref, q):
        return ref.at[pl.ds(q * CUT, CUT)]

    def own_copy():
        return pltpu.make_async_copy(packed, a_buf[0, OWN, 0].at[pl.ds(0, CAPS)], local_sem.at[4])

    class Env:
        def need(self, types, *keys):
            late = {"EF": [], "E": [], "F": []}
            for key in keys:
                full = [key]
                if key[0] == "a" and (key[3] == 1 or key[4] == 0):
                    full = [("m",) + key[1:4], key]
                for name in full:
                    todo = {}
                    for t in types:
                        k = ("own",) if t == "E" and name[0] in "am" and name[1:4] == (0, OWN, 0) else name
                        if k[0] == "b" and k[2:] == (0, 0):
                            k = ("mine", k[1])
                        if k not in waited[t]:
                            waited[t].add(k)
                            todo[t] = k
                    if len(todo) == 2 and todo["E"] == todo["F"]:
                        late["EF"].append(todo["E"])
                    else:
                        for t, k in todo.items():
                            late[t].append(k)
            for t, ks in late.items():
                if ks:

                    def waits(ks=ks):
                        for k in ks:
                            if k[0] == "mine":
                                mine(k[1]).wait()
                            else:
                                take(k)

                    when(t, waits)

        def send(self, types, key, to, refs):
            def go():
                for name, src, dst in refs():
                    put(types, name or key, src, dst, to)

            when(types, go)

        def compute(self, what, *args):
            dict(unpack=unpack, multiply=multiply, code=code)[what](*args)

        def spread(self, h, d):
            return [(None, kept.at[at_layer(d), h], b_buf.at[h, x, pl.ds(pl.multiple_of(y * PIECE, PIECE), PIECE)])]

        def across(self, h, dl):
            return [(None, kept.at[x, h] if dl == 0 else piece(h, dl, 0), piece(h, dl, 0))]

        def onward(self, h, dl, dy, part):
            return [(None, piece(h, dl, dy, part), piece(h, dl, dy, part))]

        def start(self, s, q):
            slow = [(("m", 0, s, 0), slots, m_buf[0, s, 0])] if q == 0 else []
            return slow + [(None, tiles(packed, q), tiles(a_buf[0, s, 0], q))]

        def block(self, dx, s, q, to):
            slow = [(("m", to, s, 0), m_buf[dx, s, 0], m_buf[to, s, 0])] if q == 0 else []
            return slow + [(None, tiles(a_buf[dx, s, 0], q), tiles(a_buf[to, s, 0], q))]

        def twin(self, dx, s):
            here, there = pl.ds(0, CAPS), (dx, s, 1)
            return [
                (("m", dx, s, 1), m_buf[dx, s, 0], m_buf[there]),
                (None, a_buf[dx, s, 0].at[here], a_buf[there].at[here]),
            ]

        def steps(self, h):
            return [(None, steps.at[h], steps_in.at[:, pl.ds(h * SIDE, SIDE)])]

        def part(self, h, q):
            rows = pl.ds(q * PART, PART)
            return [(None, coded.at[h, rows], coded_in.at[rows, pl.ds(h * SIDE, SIDE)])]

    def mine(h):
        return pltpu.make_async_copy(kept.at[x, h], piece(h, 0, 0), local_sem.at[2 + h])

    def unpack(dx, s):
        for dc in range(2):
            key = (dx, s, dc)
            group = lax.rem(c + dc, 2)

            def tile_row(i, carry, key=key, group=group):
                at = pl.ds(pl.multiple_of(i * TILE, TILE), TILE)
                for j in range(GROUPT):
                    slot = m_buf[key][i * GROUPT + j]
                    dense[s, dx, group, at, j * TILE : (j + 1) * TILE] = a_buf[key][slot]
                return carry

            lax.fori_loop(0, ROWT, tile_row, 0)

    def multiply(s, dl, h):
        into = partial.at[h] if s == OTHER else out.at[:, pl.ds(h * SIDE, SIDE)]
        term = jnp.dot(dense[s, dl, 0], b_buf[h, at_layer(dl), :GROUP], preferred_element_type=jnp.float32)
        term += jnp.dot(dense[s, dl, 1], b_buf[h, at_layer(dl), GROUP:], preferred_element_type=jnp.float32)
        if (s, h) in begun:
            into[...] += term
        else:
            into[...] = term
        begun.add((s, h))

    def code(h):
        for q in range(PARTS):
            part = pl.ds(q * PART, PART)
            block = partial[h, part]
            most = jnp.max(jnp.abs(block), axis=0, keepdims=True)
            some = most > SMALLEST
            steps[h, q : q + 1] = jnp.where(some, most * (1.0 / LEVELS), 0.0)
            ups = jnp.where(some, LEVELS / jnp.where(some, most, 1.0), 0.0)
            coded[h, part] = jnp.round(block * ups).astype(jnp.int32).astype(jnp.int16)

    def pack():
        def scan(i, nxt):
            t = SLOTS - 1 - i
            here = a_occ[t // GROUPT, lax.rem(t, GROUPT)] != 0
            nxt = jnp.where(here, t, nxt)
            after[t] = nxt
            return nxt

        after[SLOTS] = SLOTS - 1
        first = lax.fori_loop(0, SLOTS, scan, jnp.int32(SLOTS - 1))

        def name(t, used):
            here = a_occ[t // GROUPT, lax.rem(t, GROUPT)] != 0
            slots[t] = jnp.where(here, used, CAPS)
            return used + jnp.where(here, 1, 0)

        lax.fori_loop(0, SLOTS, name, jnp.int32(0))

        def place(s, t):
            packed[s] = a_cut[t]
            return after[t + 1]

        for t in range(SLOTS):
            i, j = divmod(t, GROUPT)
            a_cut[t] = a_in[i * TILE : (i + 1) * TILE, j * TILE : (j + 1) * TILE]

        lax.fori_loop(0, CAPS, place, first)

    for key in A_KEYS:
        a_buf[key][CAPS] = jnp.zeros((TILE, TILE), jnp.bfloat16)

    env = Env()
    get_a.wait()
    pack()
    pl.semaphore_wait(barrier, len(neighbours))
    perform(("az",), env)

    @pl.when(even)
    def _():
        own_copy().start()

        def keep_slot(t, carry):
            m_buf[0, OWN, 0][t] = slots[t]
            return carry

        lax.fori_loop(0, SLOTS, keep_slot, 0)

    get_b.wait()
    for part in range(NX):
        for i in range(BROWT):
            for k in range(COLT // NX):
                j = part * (COLT // NX) + k
                h, at = divmod(k, COLT // NX // SIDES)
                tile = b_in[i * TILE : (i + 1) * TILE, j * TILE : (j + 1) * TILE]
                present = b_occ[i, 0, j] != 0
                kept[part, h, i * TILE : (i + 1) * TILE, at * TILE : (at + 1) * TILE] = jnp.where(
                    present, tile, jnp.zeros_like(tile)
                )
    for h in range(SIDES):
        mine(h).start()

    for op in PLAN:
        perform(op, env)

    for types, copies in started.items():

        def sent(copies=copies):
            for src, dst, n, m in copies:
                remote(src, dst, n, m, beside).wait_send()

        when(types, sent)


def shards(a_tiles, a_occ, b_tiles, b_occ):
    anywhere = pl.BlockSpec(memory_space=pl.ANY)
    smem = pl.BlockSpec(memory_space=pltpu.SMEM)
    own, coded, steps = pl.pallas_call(
        product_kernel,
        out_shape=(
            jax.ShapeDtypeStruct((ROWS, NCOLS), jnp.float32),
            jax.ShapeDtypeStruct((ROWS, NCOLS), jnp.int16),
            jax.ShapeDtypeStruct((PARTS, NCOLS), jnp.float32),
        ),
        in_specs=[smem, smem, anywhere, anywhere],
        out_specs=(pl.BlockSpec(memory_space=pltpu.VMEM), anywhere, anywhere),
        scratch_shapes=[pltpu.VMEM((CAPS + 1, TILE, TILE), jnp.bfloat16)] * 16
        + [pltpu.SMEM((128,), jnp.int32)] * 16
        + [
            pltpu.VMEM((ROWS, GROUP), jnp.bfloat16),
            pltpu.VMEM((SLOTS, TILE, TILE), jnp.bfloat16),
            pltpu.VMEM((PIECE, NX * NCOLS), jnp.bfloat16),
            pltpu.VMEM((CAPS, TILE, TILE), jnp.bfloat16),
            pltpu.SMEM((128,), jnp.int32),
            pltpu.SMEM((128,), jnp.int32),
            pltpu.VMEM((NX, SIDES, PIECE, SIDE), jnp.bfloat16),
            pltpu.VMEM((SIDES, NX, NY * PIECE, SIDE), jnp.bfloat16),
            pltpu.VMEM((2, NX, 2, ROWS, GROUP), jnp.bfloat16),
            pltpu.VMEM((SIDES, ROWS, SIDE), jnp.float32),
            pltpu.VMEM((SIDES, ROWS, SIDE), jnp.int16),
            pltpu.VMEM((SIDES, PARTS, SIDE), jnp.float32),
            pltpu.SemaphoreType.DMA((200,)),
            pltpu.SemaphoreType.DMA((200,)),
            pltpu.SemaphoreType.DMA((5,)),
        ],
        compiler_params=pltpu.CompilerParams(
            collective_id=0, has_side_effects=True, vmem_limit_bytes=60 * MIB
        ),
        name="product",
    )(a_occ, b_occ.transpose(1, 0, 2), a_tiles, b_tiles)
    cut = (PARTS, PART, NCOLS)
    other = coded.reshape(cut).astype(jnp.float32) * steps[:, None, :]
    return (own.reshape(cut) + other).reshape(ROWS, NCOLS)


def solution(mesh):
    placed = (
        P("row", ("col", "layer")),
        P("row", ("col", "layer")),
        P("layer", "row", "col"),
        P("layer", "row", "col"),
    )
    return jax.shard_map(
        shards, mesh=mesh, in_specs=placed, out_specs=P("row", ("col", "layer")), check_vma=False
    )
```

```python
import jax
import jax.numpy as jnp
from jax import lax
from jax.experimental import pallas as pl
from jax.experimental.pallas import tpu as pltpu
from jax.sharding import PartitionSpec as P

MESH = pl.DeviceIdType.MESH
TILE = 128
ROWT = 8
GROUPT = 6
CAPS = 24
CUTS = 4
CUT = CAPS // CUTS
SLOTS = ROWT * GROUPT
BROWT = 3
COLT = 16
PIECE = BROWT * TILE
GROUP = GROUPT * TILE
ROWS = ROWT * TILE
NX = 4
NY = 4
NCOLS = COLT * TILE // NX
SIDES = 2
SIDE = NCOLS // SIDES
MIB = 1024 * 1024
OWN, OTHER = 0, 1
PARTS = 4
PART = ROWS // PARTS
LEVELS = 32767.0
SMALLEST = 1e-30

A_KEYS = [(dx, s, dc) for dx in range(4) for s in (OWN, OTHER) for dc in range(2)]
PLAN = [
    ("bs", 1, 2), ("by", 0, 0), ("by", 1, 0), ("bs", 0, 1), ("bs", 0, 3), ("bs", 0, 2), ("by", 1, 2), ("fq", 1),
    ("bs", 1, 3), ("by", 0, 3), ("ax", "E", 0, 1), ("ax", "F", 1, 1), ("ax", "E", 1, 1), ("ax", "F", 1, 2),
    ("fq", 0), ("bo", 1, 0), ("ac", 0, 0), ("fq", 3), ("ax", "E", 1, 0), ("by", 0, 2), ("bo", 0, 0), ("fq", 2),
    ("un", 0, 0), ("ax", "F", 1, 3), ("by", 1, 1), ("ax", "E", 1, 3), ("ax", "E", 1, 2), ("ac", 0, 1),
    ("ax", "F", 1, 0), ("by", 0, 1), ("bo", 0, 3), ("mu", 0, 0, 1), ("mu", 0, 0, 0), ("ao", "F", 1, 1), ("bs", 1, 1),
    ("un", 0, 1), ("ao", "E", 1, 3), ("ao", "F", 1, 0), ("ao", "E", 1, 0), ("ac", 3, 1), ("ao", "F", 1, 2),
    ("ax", "E", 0, 3), ("bo", 0, 2), ("un", 3, 1), ("ao", "F", 1, 3), ("av", "F", 1, 1), ("bo", 0, 1), ("bo", 1, 1),
    ("ax", "F", 0, 2), ("ac", 1, 1), ("ax", "F", 0, 0), ("ax", "E", 0, 2), ("mu", 1, 0, 0), ("un", 1, 1),
    ("av", "F", 1, 2), ("ax", "E", 0, 0), ("ax", "F", 0, 1), ("by", 1, 3), ("mu", 1, 1, 0), ("bo", 1, 2),
    ("ao", "E", 0, 1), ("ac", 2, 1), ("mu", 1, 3, 0), ("un", 2, 1), ("mu", 1, 2, 0), ("cs", 0), ("bo", 1, 3),
    ("mu", 1, 1, 1), ("ax", "F", 0, 3), ("mu", 1, 2, 1), ("ao", "F", 0, 2), ("ao", "E", 0, 3), ("ao", "F", 0, 1),
    ("mu", 1, 0, 1), ("mu", 1, 3, 1), ("ac", 1, 0), ("ao", "F", 0, 3), ("ac", 3, 0), ("ao", "F", 0, 0),
    ("ao", "E", 0, 0), ("ao", "E", 0, 2), ("cs", 1), ("un", 1, 0), ("un", 3, 0), ("mu", 0, 1, 1), ("mu", 0, 3, 0),
    ("mu", 0, 3, 1), ("cr", 0), ("ac", 2, 0), ("mu", 0, 1, 0), ("un", 2, 0), ("mu", 0, 2, 1), ("mu", 0, 2, 0),
    ("cr", 1),
]


def perform(op, env):
    kind = op[0]
    if kind == "bs":
        h, d = op[1:]
        env.send("EF", ("b", h, -d % 4, 0), dict(dx=d), lambda: env.spread(h, d))
    elif kind == "by":
        h, dl = op[1:]
        if dl:
            env.need("EF", ("b", h, dl, 0))
        for d in (1, -1):
            env.send("EF", ("b", h, dl, -d % 4), dict(dy=d), lambda: env.across(h, dl))
    elif kind == "bo":
        h, dl = op[1:]
        env.need("EF", ("b", h, dl, 3))
        env.send("EF", ("b", h, dl, 2, 0), dict(dy=1), lambda: env.onward(h, dl, -1, 0))
        env.need("EF", ("b", h, dl, 1))
        env.send("EF", ("b", h, dl, 2, 1), dict(dy=-1), lambda: env.onward(h, dl, 1, 1))
    elif kind == "az":
        for q in range(CUTS):
            env.send("E", ("a", 0, OWN, 0, q), dict(dzl=1), lambda q=q: env.start(OWN, q))
        for q in range(CUTS):
            env.send("F", ("a", 0, OTHER, 0, q), dict(dzh=1, dzl=1), lambda q=q: env.start(OTHER, q))
    elif kind == "fq":
        q = op[1]
        env.need("F", ("a", 0, OTHER, 0, q))
        env.send("F", ("a", 0, OTHER, 0, q), dict(dzl=1), lambda: env.block(0, OTHER, q, 0))
    elif kind == "ax":
        types, s, q = op[1:]
        env.need(types, ("a", 0, s, 0, q))
        for d in (1, -1):
            env.send(types, ("a", -d % 4, s, 0, q), dict(dx=d), lambda d=d: env.block(0, s, q, -d % 4))
    elif kind == "ao":
        types, s, q = op[1:]
        dx, d = (3, 1) if q < CUTS // 2 else (1, -1)
        env.need(types, ("a", dx, s, 0, q))
        env.send(types, ("a", 2, s, 0, q), dict(dx=d), lambda: env.block(dx, s, q, 2))
    elif kind == "av":
        types, s, q = op[1:]
        env.need(types, ("a", 2, s, 0, q))
        env.send(types, ("a", 2, s, 0, q), dict(dzl=1), lambda: env.block(2, s, q, 2))
    elif kind == "ac":
        dx, s = op[1:]
        for q in range(CUTS):
            env.need("EF", ("a", dx, s, 0, q))
        env.send("EF", ("a", dx, s, 1), dict(dc=1), lambda: env.twin(dx, s))
    elif kind == "un":
        dx, s = op[1:]
        for q in range(CUTS):
            env.need("EF", ("a", dx, s, 0, q))
        env.need("EF", ("a", dx, s, 1))
        env.compute("unpack", dx, s)
    elif kind == "mu":
        s, dl, h = op[1:]
        env.need("EF", ("b", h, dl, 0))
        env.need("EF", ("b", h, dl, 1), ("b", h, dl, 3), ("b", h, dl, 2, 0), ("b", h, dl, 2, 1))
        env.compute("multiply", s, dl, h)
    elif kind == "cs":
        h = op[1]
        env.compute("code", h)
        env.send("EF", ("s", h), dict(dzh=1), lambda: env.steps(h))
        for q in range(PARTS):
            env.send("EF", ("c", h, q), dict(dzh=1), lambda q=q: env.part(h, q))
    elif kind == "cr":
        h = op[1]
        env.need("EF", ("s", h))
        for q in range(PARTS):
            env.need("EF", ("c", h, q))


def product_kernel(a_occ, b_occ, a_hbm, b_hbm, out, coded_in, steps_in, *scratch):
    a_buf = dict(zip(A_KEYS, scratch[:16]))
    m_buf = dict(zip(A_KEYS, scratch[16:32]))
    (a_in, a_cut, b_in, packed, slots, after, kept, b_buf, dense, partial, coded, steps, send_sem, recv_sem, local_sem) = scratch[32:]
    row, col, x = lax.axis_index("row"), lax.axis_index("col"), lax.axis_index("layer")
    zh, y, zl, c = row // 4, lax.rem(row, 4), col // 2, lax.rem(col, 2)
    even = zh == zl
    odd = jnp.logical_not(even)

    def at_layer(dx):
        return lax.rem(x + dx + 4, 4)

    def device(dx=0, dy=0, dzh=0, dzl=0, dc=0):
        return (
            lax.rem(zh + dzh, 2) * 4 + lax.rem(y + dy + 4, 4),
            lax.rem(zl + dzl, 2) * 2 + lax.rem(c + dc, 2),
            at_layer(dx),
        )

    get_b = pltpu.make_async_copy(b_hbm.at[0], b_in, local_sem.at[0])
    get_a = pltpu.make_async_copy(a_hbm, a_in, local_sem.at[1])
    get_b.start()
    get_a.start()
    neighbours = [
        dict(dx=1), dict(dx=-1), dict(dx=2), dict(dy=1), dict(dy=-1), dict(dzl=1), dict(dzh=1), dict(dzh=1, dzl=1), dict(dc=1)
    ]
    barrier = pltpu.get_barrier_semaphore()
    for n in neighbours:
        pl.semaphore_signal(barrier, inc=1, device_id=device(**n), device_id_type=MESH)

    numbers, places, used = {}, {}, [0]
    beside = device(dx=1)
    started = {"EF": [], "E": [], "F": []}
    waited = {"E": set(), "F": set()}
    begun = set()

    def when(types, fn):
        if types == "EF":
            fn()
        else:
            pl.when(even if types == "E" else odd)(fn)

    def remote(src, dst, n, m, to):
        return pltpu.make_async_remote_copy(
            src_ref=src, dst_ref=dst, send_sem=send_sem.at[m], recv_sem=recv_sem.at[n], device_id=to, device_id_type=MESH
        )

    def put(types, key, src, dst, to):
        n = numbers.setdefault(key, len(numbers))
        m = used[0]
        used[0] += 1
        remote(src, dst, n, m, device(**to)).start()
        places[key] = dst
        started[types].append((src, dst, n, m))

    def take(key):
        if key[0] == "own":
            own_copy().wait()
            return
        n = numbers.setdefault(key, len(numbers))
        if key[0] == "a":
            dst = tiles(a_buf[key[1:4]], key[4]) if len(key) == 5 else a_buf[key[1:4]].at[pl.ds(0, CAPS)]
        elif key[0] == "m":
            dst = m_buf[key[1:4]]
        else:
            dst = places[key]
        remote(dst, dst, n, 0, beside).wait_recv()

    def piece(h, dl, dy, part=None):
        start = lax.rem(y + dy + 4, 4) * PIECE
        size = PIECE
        if part is not None:
            size = PIECE // 2
            start = start + part * size
        return b_buf.at[h, at_layer(dl), pl.ds(pl.multiple_of(start, size), size)]

    def tiles(ref, q):
        return ref.at[pl.ds(q * CUT, CUT)]

    def own_copy():
        return pltpu.make_async_copy(packed, a_buf[0, OWN, 0].at[pl.ds(0, CAPS)], local_sem.at[4])

    class Env:
        def need(self, types, *keys):
            late = {"EF": [], "E": [], "F": []}
            for key in keys:
                full = [key]
                if key[0] == "a" and (key[3] == 1 or key[4] == 0):
                    full = [("m",) + key[1:4], key]
                for name in full:
                    todo = {}
                    for t in types:
                        k = ("own",) if t == "E" and name[0] in "am" and name[1:4] == (0, OWN, 0) else name
                        if k[0] == "b" and k[2:] == (0, 0):
                            k = ("mine", k[1])
                        if k not in waited[t]:
                            waited[t].add(k)
                            todo[t] = k
                    if len(todo) == 2 and todo["E"] == todo["F"]:
                        late["EF"].append(todo["E"])
                    else:
                        for t, k in todo.items():
                            late[t].append(k)
            for t, ks in late.items():
                if ks:

                    def waits(ks=ks):
                        for k in ks:
                            if k[0] == "mine":
                                mine(k[1]).wait()
                            else:
                                take(k)

                    when(t, waits)

        def send(self, types, key, to, refs):
            def go():
                for name, src, dst in refs():
                    put(types, name or key, src, dst, to)

            when(types, go)

        def compute(self, what, *args):
            dict(unpack=unpack, multiply=multiply, code=code)[what](*args)

        def spread(self, h, d):
            return [(None, kept.at[at_layer(d), h], b_buf.at[h, x, pl.ds(pl.multiple_of(y * PIECE, PIECE), PIECE)])]

        def across(self, h, dl):
            return [(None, kept.at[x, h] if dl == 0 else piece(h, dl, 0), piece(h, dl, 0))]

        def onward(self, h, dl, dy, part):
            return [(None, piece(h, dl, dy, part), piece(h, dl, dy, part))]

        def start(self, s, q):
            slow = [(("m", 0, s, 0), slots, m_buf[0, s, 0])] if q == 0 else []
            return slow + [(None, tiles(packed, q), tiles(a_buf[0, s, 0], q))]

        def block(self, dx, s, q, to):
            slow = [(("m", to, s, 0), m_buf[dx, s, 0], m_buf[to, s, 0])] if q == 0 else []
            return slow + [(None, tiles(a_buf[dx, s, 0], q), tiles(a_buf[to, s, 0], q))]

        def twin(self, dx, s):
            here, there = pl.ds(0, CAPS), (dx, s, 1)
            return [
                (("m", dx, s, 1), m_buf[dx, s, 0], m_buf[there]),
                (None, a_buf[dx, s, 0].at[here], a_buf[there].at[here]),
            ]

        def steps(self, h):
            return [(None, steps.at[h], steps_in.at[:, pl.ds(h * SIDE, SIDE)])]

        def part(self, h, q):
            rows = pl.ds(q * PART, PART)
            return [(None, coded.at[h, rows], coded_in.at[rows, pl.ds(h * SIDE, SIDE)])]

    def mine(h):
        return pltpu.make_async_copy(kept.at[x, h], piece(h, 0, 0), local_sem.at[2 + h])

    def unpack(dx, s):
        for dc in range(2):
            key = (dx, s, dc)
            group = lax.rem(c + dc, 2)

            def tile_row(i, carry, key=key, group=group):
                at = pl.ds(pl.multiple_of(i * TILE, TILE), TILE)
                for j in range(GROUPT):
                    slot = m_buf[key][i * GROUPT + j]
                    across = pl.ds(pl.multiple_of(group * GROUP + j * TILE, TILE), TILE)
                    dense[s, dx, at, across] = a_buf[key][slot]
                return carry

            lax.fori_loop(0, ROWT, tile_row, 0, unroll=True)

    def multiply(s, dl, h):
        into = partial.at[h] if s == OTHER else out.at[:, pl.ds(h * SIDE, SIDE)]
        for m in range(4):
            at = pl.ds(m * (ROWS // 4), ROWS // 4)
            term = jnp.dot(dense[s, dl, at], b_buf[h, at_layer(dl)], preferred_element_type=jnp.float32)
            if (s, h) in begun:
                into[at] += term
            else:
                into[at] = term
        begun.add((s, h))

    def code(h):
        for q in range(PARTS):
            part = pl.ds(q * PART, PART)
            block = partial[h, part]
            most = jnp.max(jnp.abs(block), axis=0, keepdims=True)
            some = most > SMALLEST
            steps[h, q : q + 1] = jnp.where(some, most * (1.0 / LEVELS), 0.0)
            ups = jnp.where(some, LEVELS / jnp.where(some, most, 1.0), 0.0)
            coded[h, part] = jnp.round(block * ups).astype(jnp.int32).astype(jnp.int16)

    def pack():
        def scan(i, nxt):
            t = SLOTS - 1 - i
            here = a_occ[t // GROUPT, lax.rem(t, GROUPT)] != 0
            nxt = jnp.where(here, t, nxt)
            after[t] = nxt
            return nxt

        after[SLOTS] = SLOTS - 1
        first = lax.fori_loop(0, SLOTS, scan, jnp.int32(SLOTS - 1))

        def name(t, used):
            here = a_occ[t // GROUPT, lax.rem(t, GROUPT)] != 0
            slots[t] = jnp.where(here, used, CAPS)
            return used + jnp.where(here, 1, 0)

        lax.fori_loop(0, SLOTS, name, jnp.int32(0))

        def place(s, t):
            packed[s] = a_cut[t]
            return after[t + 1]

        for t in range(SLOTS):
            i, j = divmod(t, GROUPT)
            a_cut[t] = a_in[i * TILE : (i + 1) * TILE, j * TILE : (j + 1) * TILE]

        lax.fori_loop(0, CAPS, place, first)

    for key in A_KEYS:
        a_buf[key][CAPS] = jnp.zeros((TILE, TILE), jnp.bfloat16)

    env = Env()
    get_a.wait()
    pack()
    pl.semaphore_wait(barrier, len(neighbours))
    perform(("az",), env)

    @pl.when(even)
    def _():
        own_copy().start()

        def keep_slot(t, carry):
            m_buf[0, OWN, 0][t] = slots[t]
            return carry

        lax.fori_loop(0, SLOTS, keep_slot, 0)

    get_b.wait()
    for part in range(NX):
        for i in range(BROWT):
            for k in range(COLT // NX):
                j = part * (COLT // NX) + k
                h, at = divmod(k, COLT // NX // SIDES)
                tile = b_in[i * TILE : (i + 1) * TILE, j * TILE : (j + 1) * TILE]
                present = b_occ[i, 0, j] != 0
                kept[part, h, i * TILE : (i + 1) * TILE, at * TILE : (at + 1) * TILE] = jnp.where(
                    present, tile, jnp.zeros_like(tile)
                )
    for h in range(SIDES):
        mine(h).start()

    for op in PLAN:
        perform(op, env)

    for types, copies in started.items():

        def sent(copies=copies):
            for src, dst, n, m in copies:
                remote(src, dst, n, m, beside).wait_send()

        when(types, sent)


def shards(a_tiles, a_occ, b_tiles, b_occ):
    anywhere = pl.BlockSpec(memory_space=pl.ANY)
    smem = pl.BlockSpec(memory_space=pltpu.SMEM)
    own, coded, steps = pl.pallas_call(
        product_kernel,
        out_shape=(
            jax.ShapeDtypeStruct((ROWS, NCOLS), jnp.float32),
            jax.ShapeDtypeStruct((ROWS, NCOLS), jnp.int16),
            jax.ShapeDtypeStruct((PARTS, NCOLS), jnp.float32),
        ),
        in_specs=[smem, smem, anywhere, anywhere],
        out_specs=(pl.BlockSpec(memory_space=pltpu.VMEM), anywhere, anywhere),
        scratch_shapes=[pltpu.VMEM((CAPS + 1, TILE, TILE), jnp.bfloat16)] * 16
        + [pltpu.SMEM((128,), jnp.int32)] * 16
        + [
            pltpu.VMEM((ROWS, GROUP), jnp.bfloat16),
            pltpu.VMEM((SLOTS, TILE, TILE), jnp.bfloat16),
            pltpu.VMEM((PIECE, NX * NCOLS), jnp.bfloat16),
            pltpu.VMEM((CAPS, TILE, TILE), jnp.bfloat16),
            pltpu.SMEM((128,), jnp.int32),
            pltpu.SMEM((128,), jnp.int32),
            pltpu.VMEM((NX, SIDES, PIECE, SIDE), jnp.bfloat16),
            pltpu.VMEM((SIDES, NX, NY * PIECE, SIDE), jnp.bfloat16),
            pltpu.VMEM((2, NX, ROWS, 2 * GROUP), jnp.bfloat16),
            pltpu.VMEM((SIDES, ROWS, SIDE), jnp.float32),
            pltpu.VMEM((SIDES, ROWS, SIDE), jnp.int16),
            pltpu.VMEM((SIDES, PARTS, SIDE), jnp.float32),
            pltpu.SemaphoreType.DMA((200,)),
            pltpu.SemaphoreType.DMA((200,)),
            pltpu.SemaphoreType.DMA((5,)),
        ],
        compiler_params=pltpu.CompilerParams(
            collective_id=0, has_side_effects=True, vmem_limit_bytes=60 * MIB
        ),
        name="product",
    )(a_occ, b_occ.transpose(1, 0, 2), a_tiles, b_tiles)
    cut = (PARTS, PART, NCOLS)
    other = coded.reshape(cut).astype(jnp.float32) * steps[:, None, :]
    return (own.reshape(cut) + other).reshape(ROWS, NCOLS)


def solution(mesh):
    placed = (
        P("row", ("col", "layer")),
        P("row", ("col", "layer")),
        P("layer", "row", "col"),
        P("layer", "row", "col"),
    )
    return jax.shard_map(
        shards, mesh=mesh, in_specs=placed, out_specs=P("row", ("col", "layer")), check_vma=False
    )
```

```python
import jax
import jax.numpy as jnp
from jax import lax
from jax.experimental import pallas as pl
from jax.experimental.pallas import tpu as pltpu
from jax.sharding import PartitionSpec as P

MESH = pl.DeviceIdType.MESH
TILE = 128
ROWT = 8
GROUPT = 6
CAPS = 24
CUTS = 4
CUT = CAPS // CUTS
SLOTS = ROWT * GROUPT
BROWT = 3
COLT = 16
PIECE = BROWT * TILE
GROUP = GROUPT * TILE
ROWS = ROWT * TILE
NX = 4
NY = 4
NCOLS = COLT * TILE // NX
SIDES = 2
SIDE = NCOLS // SIDES
MIB = 1024 * 1024
OWN, OTHER = 0, 1
PARTS = 4
PART = ROWS // PARTS
LEVELS = 32767.0
SMALLEST = 1e-30

A_KEYS = [(dx, s, dc) for dx in range(4) for s in (OWN, OTHER) for dc in range(2)]
PLAN = [
    ("bs", 1, 2), ("by", 0, 0), ("by", 1, 0), ("bs", 0, 1), ("bs", 0, 3), ("bs", 0, 2), ("by", 1, 2), ("fq", 1),
    ("bs", 1, 3), ("by", 0, 3), ("ax", "E", 0, 1), ("ax", "F", 1, 1), ("ax", "E", 1, 1), ("ax", "F", 1, 2),
    ("fq", 0), ("bo", 1, 0), ("ac", 0, 0), ("fq", 3), ("ax", "E", 1, 0), ("by", 0, 2), ("bo", 0, 0), ("fq", 2),
    ("un", 0, 0), ("ax", "F", 1, 3), ("by", 1, 1), ("ax", "E", 1, 3), ("ax", "E", 1, 2), ("ac", 0, 1),
    ("ax", "F", 1, 0), ("by", 0, 1), ("bo", 0, 3), ("mu", 0, 0, 1), ("mu", 0, 0, 0), ("ao", "F", 1, 1), ("bs", 1, 1),
    ("un", 0, 1), ("ao", "E", 1, 3), ("ao", "F", 1, 0), ("ao", "E", 1, 0), ("ac", 3, 1), ("ao", "F", 1, 2),
    ("ax", "E", 0, 3), ("bo", 0, 2), ("un", 3, 1), ("ao", "F", 1, 3), ("av", "F", 1, 1), ("bo", 0, 1), ("bo", 1, 1),
    ("ax", "F", 0, 2), ("ac", 1, 1), ("ax", "F", 0, 0), ("ax", "E", 0, 2), ("mu", 1, 0, 0), ("un", 1, 1),
    ("av", "F", 1, 2), ("ax", "E", 0, 0), ("ax", "F", 0, 1), ("by", 1, 3), ("mu", 1, 1, 0), ("bo", 1, 2),
    ("ao", "E", 0, 1), ("ac", 2, 1), ("mu", 1, 3, 0), ("un", 2, 1), ("mu", 1, 2, 0), ("cs", 0), ("bo", 1, 3),
    ("mu", 1, 1, 1), ("ax", "F", 0, 3), ("mu", 1, 2, 1), ("ao", "F", 0, 2), ("ao", "E", 0, 3), ("ao", "F", 0, 1),
    ("mu", 1, 0, 1), ("mu", 1, 3, 1), ("ac", 1, 0), ("ao", "F", 0, 3), ("ac", 3, 0), ("ao", "F", 0, 0),
    ("ao", "E", 0, 0), ("ao", "E", 0, 2), ("cs", 1), ("un", 1, 0), ("un", 3, 0), ("mu", 0, 1, 1), ("mu", 0, 3, 0),
    ("mu", 0, 3, 1), ("cr", 0), ("ac", 2, 0), ("mu", 0, 1, 0), ("un", 2, 0), ("mu", 0, 2, 1), ("mu", 0, 2, 0),
    ("cr", 1),
]


def perform(op, env):
    kind = op[0]
    if kind == "bs":
        h, d = op[1:]
        env.send("EF", ("b", h, -d % 4, 0), dict(dx=d), lambda: env.spread(h, d))
    elif kind == "by":
        h, dl = op[1:]
        if dl:
            env.need("EF", ("b", h, dl, 0))
        for d in (1, -1):
            env.send("EF", ("b", h, dl, -d % 4), dict(dy=d), lambda: env.across(h, dl))
    elif kind == "bo":
        h, dl = op[1:]
        env.need("EF", ("b", h, dl, 3))
        env.send("EF", ("b", h, dl, 2, 0), dict(dy=1), lambda: env.onward(h, dl, -1, 0))
        env.need("EF", ("b", h, dl, 1))
        env.send("EF", ("b", h, dl, 2, 1), dict(dy=-1), lambda: env.onward(h, dl, 1, 1))
    elif kind == "az":
        for q in range(CUTS):
            env.send("E", ("a", 0, OWN, 0, q), dict(dzl=1), lambda q=q: env.start(OWN, q))
        for q in range(CUTS):
            env.send("F", ("a", 0, OTHER, 0, q), dict(dzh=1, dzl=1), lambda q=q: env.start(OTHER, q))
    elif kind == "fq":
        q = op[1]
        env.need("F", ("a", 0, OTHER, 0, q))
        env.send("F", ("a", 0, OTHER, 0, q), dict(dzl=1), lambda: env.block(0, OTHER, q, 0))
    elif kind == "ax":
        types, s, q = op[1:]
        env.need(types, ("a", 0, s, 0, q))
        for d in (1, -1):
            env.send(types, ("a", -d % 4, s, 0, q), dict(dx=d), lambda d=d: env.block(0, s, q, -d % 4))
    elif kind == "ao":
        types, s, q = op[1:]
        dx, d = (3, 1) if q < CUTS // 2 else (1, -1)
        env.need(types, ("a", dx, s, 0, q))
        env.send(types, ("a", 2, s, 0, q), dict(dx=d), lambda: env.block(dx, s, q, 2))
    elif kind == "av":
        types, s, q = op[1:]
        env.need(types, ("a", 2, s, 0, q))
        env.send(types, ("a", 2, s, 0, q), dict(dzl=1), lambda: env.block(2, s, q, 2))
    elif kind == "ac":
        dx, s = op[1:]
        for q in range(CUTS):
            env.need("EF", ("a", dx, s, 0, q))
        env.send("EF", ("a", dx, s, 1), dict(dc=1), lambda: env.twin(dx, s))
    elif kind == "un":
        dx, s = op[1:]
        for q in range(CUTS):
            env.need("EF", ("a", dx, s, 0, q))
        env.need("EF", ("a", dx, s, 1))
        env.compute("unpack", dx, s)
    elif kind == "mu":
        s, dl, h = op[1:]
        env.need("EF", ("b", h, dl, 0))
        env.need("EF", ("b", h, dl, 1), ("b", h, dl, 3), ("b", h, dl, 2, 0), ("b", h, dl, 2, 1))
        env.compute("multiply", s, dl, h)
    elif kind == "cs":
        h = op[1]
        env.compute("code", h)
        env.send("EF", ("s", h), dict(dzh=1), lambda: env.steps(h))
        for q in range(PARTS):
            env.send("EF", ("c", h, q), dict(dzh=1), lambda q=q: env.part(h, q))
    elif kind == "cr":
        h = op[1]
        env.need("EF", ("s", h))
        for q in range(PARTS):
            env.need("EF", ("c", h, q))


def product_kernel(a_occ, b_occ, a_hbm, b_hbm, out, coded_in, steps_in, *scratch):
    a_buf = dict(zip(A_KEYS, scratch[:16]))
    m_buf = dict(zip(A_KEYS, scratch[16:32]))
    (a_in, a_cut, b_in, packed, slots, after, kept, b_buf, dense, partial, coded, steps, send_sem, recv_sem, local_sem) = scratch[32:]
    row, col, x = lax.axis_index("row"), lax.axis_index("col"), lax.axis_index("layer")
    zh, y, zl, c = row // 4, lax.rem(row, 4), col // 2, lax.rem(col, 2)
    even = zh == zl
    odd = jnp.logical_not(even)

    def at_layer(dx):
        return lax.rem(x + dx + 4, 4)

    def device(dx=0, dy=0, dzh=0, dzl=0, dc=0):
        return (
            lax.rem(zh + dzh, 2) * 4 + lax.rem(y + dy + 4, 4),
            lax.rem(zl + dzl, 2) * 2 + lax.rem(c + dc, 2),
            at_layer(dx),
        )

    get_b = pltpu.make_async_copy(b_hbm.at[0], b_in, local_sem.at[0])
    get_a = pltpu.make_async_copy(a_hbm, a_in, local_sem.at[1])
    get_b.start()
    get_a.start()
    neighbours = [
        dict(dx=1), dict(dx=-1), dict(dx=2), dict(dy=1), dict(dy=-1), dict(dzl=1), dict(dzh=1), dict(dzh=1, dzl=1), dict(dc=1)
    ]
    barrier = pltpu.get_barrier_semaphore()
    for n in neighbours:
        pl.semaphore_signal(barrier, inc=1, device_id=device(**n), device_id_type=MESH)

    numbers, places, used = {}, {}, [0]
    beside = device(dx=1)
    started = {"EF": [], "E": [], "F": []}
    waited = {"E": set(), "F": set()}
    begun = set()

    def when(types, fn):
        if types == "EF":
            fn()
        else:
            pl.when(even if types == "E" else odd)(fn)

    def remote(src, dst, n, m, to):
        return pltpu.make_async_remote_copy(
            src_ref=src, dst_ref=dst, send_sem=send_sem.at[m], recv_sem=recv_sem.at[n], device_id=to, device_id_type=MESH
        )

    def put(types, key, src, dst, to):
        n = numbers.setdefault(key, len(numbers))
        m = used[0]
        used[0] += 1
        remote(src, dst, n, m, device(**to)).start()
        places[key] = dst
        started[types].append((src, dst, n, m))

    def take(key):
        if key[0] == "own":
            own_copy().wait()
            return
        n = numbers.setdefault(key, len(numbers))
        if key[0] == "a":
            dst = tiles(a_buf[key[1:4]], key[4]) if len(key) == 5 else a_buf[key[1:4]].at[pl.ds(0, CAPS)]
        elif key[0] == "m":
            dst = m_buf[key[1:4]]
        else:
            dst = places[key]
        remote(dst, dst, n, 0, beside).wait_recv()

    def piece(h, dl, dy, part=None):
        start = lax.rem(y + dy + 4, 4) * PIECE
        size = PIECE
        if part is not None:
            size = PIECE // 2
            start = start + part * size
        return b_buf.at[h, at_layer(dl), pl.ds(pl.multiple_of(start, size), size)]

    def tiles(ref, q):
        return ref.at[pl.ds(q * CUT, CUT)]

    def own_copy():
        return pltpu.make_async_copy(packed, a_buf[0, OWN, 0].at[pl.ds(0, CAPS)], local_sem.at[4])

    class Env:
        def need(self, types, *keys):
            late = {"EF": [], "E": [], "F": []}
            for key in keys:
                full = [key]
                if key[0] == "a" and (key[3] == 1 or key[4] == 0):
                    full = [("m",) + key[1:4], key]
                for name in full:
                    todo = {}
                    for t in types:
                        k = ("own",) if t == "E" and name[0] in "am" and name[1:4] == (0, OWN, 0) else name
                        if k[0] == "b" and k[2:] == (0, 0):
                            k = ("mine", k[1])
                        if k not in waited[t]:
                            waited[t].add(k)
                            todo[t] = k
                    if len(todo) == 2 and todo["E"] == todo["F"]:
                        late["EF"].append(todo["E"])
                    else:
                        for t, k in todo.items():
                            late[t].append(k)
            for t, ks in late.items():
                if ks:

                    def waits(ks=ks):
                        for k in ks:
                            if k[0] == "mine":
                                mine(k[1]).wait()
                            else:
                                take(k)

                    when(t, waits)

        def send(self, types, key, to, refs):
            def go():
                for name, src, dst in refs():
                    put(types, name or key, src, dst, to)

            when(types, go)

        def compute(self, what, *args):
            dict(unpack=unpack, multiply=multiply, code=code)[what](*args)

        def spread(self, h, d):
            return [(None, kept.at[at_layer(d), h], b_buf.at[h, x, pl.ds(pl.multiple_of(y * PIECE, PIECE), PIECE)])]

        def across(self, h, dl):
            return [(None, kept.at[x, h] if dl == 0 else piece(h, dl, 0), piece(h, dl, 0))]

        def onward(self, h, dl, dy, part):
            return [(None, piece(h, dl, dy, part), piece(h, dl, dy, part))]

        def start(self, s, q):
            slow = [(("m", 0, s, 0), slots, m_buf[0, s, 0])] if q == 0 else []
            return slow + [(None, tiles(packed, q), tiles(a_buf[0, s, 0], q))]

        def block(self, dx, s, q, to):
            slow = [(("m", to, s, 0), m_buf[dx, s, 0], m_buf[to, s, 0])] if q == 0 else []
            return slow + [(None, tiles(a_buf[dx, s, 0], q), tiles(a_buf[to, s, 0], q))]

        def twin(self, dx, s):
            here, there = pl.ds(0, CAPS), (dx, s, 1)
            return [
                (("m", dx, s, 1), m_buf[dx, s, 0], m_buf[there]),
                (None, a_buf[dx, s, 0].at[here], a_buf[there].at[here]),
            ]

        def steps(self, h):
            return [(None, steps.at[h], steps_in.at[:, pl.ds(h * SIDE, SIDE)])]

        def part(self, h, q):
            rows = pl.ds(q * PART, PART)
            return [(None, coded.at[h, rows], coded_in.at[rows, pl.ds(h * SIDE, SIDE)])]

    def mine(h):
        return pltpu.make_async_copy(kept.at[x, h], piece(h, 0, 0), local_sem.at[2 + h])

    def unpack(dx, s):
        for dc in range(2):
            key = (dx, s, dc)
            group = lax.rem(c + dc, 2)

            def tile_row(i, carry, key=key, group=group):
                at = pl.ds(pl.multiple_of(i * TILE, TILE), TILE)
                for j in range(GROUPT):
                    slot = m_buf[key][i * GROUPT + j]
                    across = pl.ds(pl.multiple_of(group * GROUP + j * TILE, TILE), TILE)
                    dense[s, dx, at, across] = a_buf[key][slot]
                return carry

            lax.fori_loop(0, ROWT, tile_row, 0, unroll=True)

    def multiply(s, dl, h):
        into = partial.at[h] if s == OTHER else out.at[:, pl.ds(h * SIDE, SIDE)]
        for m in range(4):
            at = pl.ds(m * (ROWS // 4), ROWS // 4)
            term = jnp.dot(dense[s, dl, at], b_buf[h, at_layer(dl)], preferred_element_type=jnp.float32)
            if (s, h) in begun:
                into[at] += term
            else:
                into[at] = term
        begun.add((s, h))

    def code(h):
        for q in range(PARTS):
            part = pl.ds(q * PART, PART)
            block = partial[h, part]
            most = jnp.max(jnp.abs(block), axis=0, keepdims=True)
            some = most > SMALLEST
            steps[h, q : q + 1] = jnp.where(some, most * (1.0 / LEVELS), 0.0)
            ups = jnp.where(some, LEVELS / jnp.where(some, most, 1.0), 0.0)
            coded[h, part] = jnp.round(block * ups).astype(jnp.int32).astype(jnp.int16)

    def pack():
        def scan(i, nxt):
            t = SLOTS - 1 - i
            here = a_occ[t // GROUPT, lax.rem(t, GROUPT)] != 0
            nxt = jnp.where(here, t, nxt)
            after[t] = nxt
            return nxt

        after[SLOTS] = SLOTS - 1
        first = lax.fori_loop(0, SLOTS, scan, jnp.int32(SLOTS - 1))

        def name(t, used):
            here = a_occ[t // GROUPT, lax.rem(t, GROUPT)] != 0
            slots[t] = jnp.where(here, used, CAPS)
            return used + jnp.where(here, 1, 0)

        lax.fori_loop(0, SLOTS, name, jnp.int32(0))

        def place(s, t):
            packed[s] = a_cut[t]
            return after[t + 1]

        for t in range(SLOTS):
            i, j = divmod(t, GROUPT)
            a_cut[t] = a_in[i * TILE : (i + 1) * TILE, j * TILE : (j + 1) * TILE]

        lax.fori_loop(0, CAPS, place, first)

    for key in A_KEYS:
        a_buf[key][CAPS] = jnp.zeros((TILE, TILE), jnp.bfloat16)

    env = Env()
    get_a.wait()
    pack()
    pl.semaphore_wait(barrier, len(neighbours))
    perform(("az",), env)

    @pl.when(even)
    def _():
        own_copy().start()

        def keep_slot(t, carry):
            m_buf[0, OWN, 0][t] = slots[t]
            return carry

        lax.fori_loop(0, SLOTS, keep_slot, 0)

    get_b.wait()
    for part in range(NX):
        for i in range(BROWT):
            for k in range(COLT // NX):
                j = part * (COLT // NX) + k
                h, at = divmod(k, COLT // NX // SIDES)
                tile = b_in[i * TILE : (i + 1) * TILE, j * TILE : (j + 1) * TILE]
                present = b_occ[i, 0, j] != 0
                kept[part, h, i * TILE : (i + 1) * TILE, at * TILE : (at + 1) * TILE] = jnp.where(
                    present, tile, jnp.zeros_like(tile)
                )
    for h in range(SIDES):
        mine(h).start()

    for op in PLAN:
        perform(op, env)

    for types, copies in started.items():

        def sent(copies=copies):
            for src, dst, n, m in copies:
                remote(src, dst, n, m, beside).wait_send()

        when(types, sent)


def add_kernel(own, coded, steps, out):
    i = pl.program_id(0)
    out[...] = own[...] + coded[...].astype(jnp.float32) * steps[pl.ds(i, 1)]


def shards(a_tiles, a_occ, b_tiles, b_occ):
    anywhere = pl.BlockSpec(memory_space=pl.ANY)
    smem = pl.BlockSpec(memory_space=pltpu.SMEM)
    own, coded, steps = pl.pallas_call(
        product_kernel,
        out_shape=(
            jax.ShapeDtypeStruct((ROWS, NCOLS), jnp.float32),
            jax.ShapeDtypeStruct((ROWS, NCOLS), jnp.int16),
            jax.ShapeDtypeStruct((PARTS, NCOLS), jnp.float32),
        ),
        in_specs=[smem, smem, anywhere, anywhere],
        out_specs=(pl.BlockSpec(memory_space=pltpu.VMEM), anywhere, anywhere),
        scratch_shapes=[pltpu.VMEM((CAPS + 1, TILE, TILE), jnp.bfloat16)] * 16
        + [pltpu.SMEM((128,), jnp.int32)] * 16
        + [
            pltpu.VMEM((ROWS, GROUP), jnp.bfloat16),
            pltpu.VMEM((SLOTS, TILE, TILE), jnp.bfloat16),
            pltpu.VMEM((PIECE, NX * NCOLS), jnp.bfloat16),
            pltpu.VMEM((CAPS, TILE, TILE), jnp.bfloat16),
            pltpu.SMEM((128,), jnp.int32),
            pltpu.SMEM((128,), jnp.int32),
            pltpu.VMEM((NX, SIDES, PIECE, SIDE), jnp.bfloat16),
            pltpu.VMEM((SIDES, NX, NY * PIECE, SIDE), jnp.bfloat16),
            pltpu.VMEM((2, NX, ROWS, 2 * GROUP), jnp.bfloat16),
            pltpu.VMEM((SIDES, ROWS, SIDE), jnp.float32),
            pltpu.VMEM((SIDES, ROWS, SIDE), jnp.int16),
            pltpu.VMEM((SIDES, PARTS, SIDE), jnp.float32),
            pltpu.SemaphoreType.DMA((200,)),
            pltpu.SemaphoreType.DMA((200,)),
            pltpu.SemaphoreType.DMA((5,)),
        ],
        compiler_params=pltpu.CompilerParams(
            collective_id=0, has_side_effects=True, vmem_limit_bytes=60 * MIB
        ),
        name="product",
    )(a_occ, b_occ.transpose(1, 0, 2), a_tiles, b_tiles)
    by_part = pl.BlockSpec((PART, NCOLS), lambda i: (i, 0))
    return pl.pallas_call(
        add_kernel,
        grid=(PARTS,),
        out_shape=jax.ShapeDtypeStruct((ROWS, NCOLS), jnp.float32),
        in_specs=[by_part, by_part, pl.BlockSpec((PARTS, NCOLS), lambda i: (0, 0))],
        out_specs=by_part,
        compiler_params=pltpu.CompilerParams(vmem_limit_bytes=60 * MIB),
        name="add",
    )(own, coded, steps)


def solution(mesh):
    placed = (
        P("row", ("col", "layer")),
        P("row", ("col", "layer")),
        P("layer", "row", "col"),
        P("layer", "row", "col"),
    )
    return jax.shard_map(
        shards, mesh=mesh, in_specs=placed, out_specs=P("row", ("col", "layer")), check_vma=False
    )
```

```python
import jax
import jax.numpy as jnp
from jax import lax
from jax.experimental import pallas as pl
from jax.experimental.pallas import tpu as pltpu
from jax.sharding import PartitionSpec as P

MESH = pl.DeviceIdType.MESH
TILE = 128
ROWT = 8
GROUPT = 6
CAPS = 24
CUTS = 4
CUT = CAPS // CUTS
SLOTS = ROWT * GROUPT
BROWT = 3
COLT = 16
PIECE = BROWT * TILE
GROUP = GROUPT * TILE
ROWS = ROWT * TILE
NX = 4
NY = 4
NCOLS = COLT * TILE // NX
SIDES = 2
SIDE = NCOLS // SIDES
MIB = 1024 * 1024
OWN, OTHER = 0, 1
PARTS = 4
PART = ROWS // PARTS
LEVELS = 32767.0
SMALLEST = 1e-30

A_KEYS = [(dx, s, dc) for dx in range(4) for s in (OWN, OTHER) for dc in range(2)]
PLAN = [
    ("bs", 0, 2), ("bs", 1, 3), ("bs", 0, 1), ("by", 0, 0), ("bs", 1, 1), ("bs", 0, 3), ("by", 1, 0), ("fq", 0),
    ("by", 0, 2), ("ax", "F", 1, 0), ("fq", 1), ("fq", 2), ("ax", "E", 1, 0), ("bs", 1, 2), ("bo", 0, 0),
    ("by", 0, 3), ("by", 0, 1), ("ao", "F", 1, 0), ("ax", "E", 1, 1), ("ax", "E", 1, 2), ("by", 1, 3), ("bo", 1, 0),
    ("ax", "F", 1, 3), ("ax", "E", 1, 3), ("fq", 3), ("bo", 0, 3), ("ax", "F", 1, 2), ("ac", 0, 0), ("ac", 0, 1),
    ("un", 0, 1), ("ao", "F", 1, 3), ("un", 0, 0), ("bo", 0, 2), ("bo", 0, 1), ("av", "F", 1, 0), ("bo", 1, 3),
    ("ao", "F", 1, 2), ("ao", "E", 1, 1), ("ao", "E", 1, 2), ("ax", "E", 0, 2), ("ax", "F", 1, 1), ("ax", "F", 0, 0),
    ("ax", "E", 0, 0), ("av", "F", 1, 3), ("mu", 1, 0, 1), ("by", 1, 2), ("mu", 1, 0, 0), ("ac", 3, 1),
    ("ao", "F", 1, 1), ("by", 1, 1), ("un", 3, 1), ("ax", "F", 0, 1), ("ax", "E", 0, 1), ("ac", 1, 1),
    ("ax", "F", 0, 3), ("mu", 1, 3, 0), ("ax", "E", 0, 3), ("un", 1, 1), ("mu", 1, 1, 0), ("ac", 2, 1),
    ("mu", 0, 0, 1), ("ax", "F", 0, 2), ("un", 2, 1), ("bo", 1, 2), ("mu", 1, 2, 0), ("cs", 0), ("ao", "F", 0, 0),
    ("ao", "E", 0, 2), ("mu", 0, 0, 0), ("bo", 1, 1), ("mu", 1, 2, 1), ("ao", "F", 0, 3), ("ao", "F", 0, 1),
    ("ao", "E", 0, 0), ("ao", "E", 0, 1), ("mu", 1, 3, 1), ("mu", 1, 1, 1), ("ac", 3, 0), ("ao", "F", 0, 2),
    ("cs", 1), ("ao", "E", 0, 3), ("ac", 1, 0), ("un", 3, 0), ("un", 1, 0), ("cr", 0), ("mu", 0, 3, 0),
    ("mu", 0, 3, 1), ("mu", 0, 1, 1), ("ac", 2, 0), ("mu", 0, 1, 0), ("un", 2, 0), ("mu", 0, 2, 0), ("mu", 0, 2, 1),
    ("cr", 1),
]


def perform(op, env):
    kind = op[0]
    if kind == "bs":
        h, d = op[1:]
        env.send("EF", ("b", h, -d % 4, 0), dict(dx=d), lambda: env.spread(h, d))
    elif kind == "by":
        h, dl = op[1:]
        if dl:
            env.need("EF", ("b", h, dl, 0))
        for d in (1, -1):
            env.send("EF", ("b", h, dl, -d % 4), dict(dy=d), lambda: env.across(h, dl))
    elif kind == "bo":
        h, dl = op[1:]
        env.need("EF", ("b", h, dl, 3))
        env.send("EF", ("b", h, dl, 2, 0), dict(dy=1), lambda: env.onward(h, dl, -1, 0))
        env.need("EF", ("b", h, dl, 1))
        env.send("EF", ("b", h, dl, 2, 1), dict(dy=-1), lambda: env.onward(h, dl, 1, 1))
    elif kind == "az":
        for q in range(CUTS):
            env.send("E", ("a", 0, OWN, 0, q), dict(dzl=1), lambda q=q: env.start(OWN, q))
        for q in range(CUTS):
            env.send("F", ("a", 0, OTHER, 0, q), dict(dzh=1, dzl=1), lambda q=q: env.start(OTHER, q))
    elif kind == "fq":
        q = op[1]
        env.need("F", ("a", 0, OTHER, 0, q))
        env.send("F", ("a", 0, OTHER, 0, q), dict(dzl=1), lambda: env.block(0, OTHER, q, 0))
    elif kind == "ax":
        types, s, q = op[1:]
        env.need(types, ("a", 0, s, 0, q))
        for d in (1, -1):
            env.send(types, ("a", -d % 4, s, 0, q), dict(dx=d), lambda d=d: env.block(0, s, q, -d % 4))
    elif kind == "ao":
        types, s, q = op[1:]
        dx, d = (3, 1) if q < CUTS // 2 else (1, -1)
        env.need(types, ("a", dx, s, 0, q))
        env.send(types, ("a", 2, s, 0, q), dict(dx=d), lambda: env.block(dx, s, q, 2))
    elif kind == "av":
        types, s, q = op[1:]
        env.need(types, ("a", 2, s, 0, q))
        env.send(types, ("a", 2, s, 0, q), dict(dzl=1), lambda: env.block(2, s, q, 2))
    elif kind == "ac":
        dx, s = op[1:]
        for q in range(CUTS):
            env.need("EF", ("a", dx, s, 0, q))
        env.send("EF", ("a", dx, s, 1), dict(dc=1), lambda: env.twin(dx, s))
    elif kind == "un":
        dx, s = op[1:]
        for q in range(CUTS):
            env.need("EF", ("a", dx, s, 0, q))
        env.need("EF", ("a", dx, s, 1))
        env.compute("unpack", dx, s)
    elif kind == "mu":
        s, dl, h = op[1:]
        env.need("EF", ("b", h, dl, 0))
        env.need("EF", ("b", h, dl, 1), ("b", h, dl, 3), ("b", h, dl, 2, 0), ("b", h, dl, 2, 1))
        env.compute("multiply", s, dl, h)
    elif kind == "cs":
        h = op[1]
        env.compute("code", h)
        env.send("EF", ("s", h), dict(dzh=1), lambda: env.steps(h))
        for q in range(PARTS):
            env.send("EF", ("c", h, q), dict(dzh=1), lambda q=q: env.part(h, q))
    elif kind == "cr":
        h = op[1]
        env.need("EF", ("s", h))
        for q in range(PARTS):
            env.need("EF", ("c", h, q))


def product_kernel(a_occ, b_occ, a_hbm, b_hbm, out, coded_in, steps_in, *scratch):
    a_buf = dict(zip(A_KEYS, scratch[:16]))
    m_buf = dict(zip(A_KEYS, scratch[16:32]))
    (a_in, a_cut, b_in, packed, slots, after, kept, b_buf, dense, partial, coded, steps, send_sem, recv_sem, local_sem) = scratch[32:]
    row, col, x = lax.axis_index("row"), lax.axis_index("col"), lax.axis_index("layer")
    zh, y, zl, c = row // 4, lax.rem(row, 4), col // 2, lax.rem(col, 2)
    even = zh == zl
    odd = jnp.logical_not(even)

    def at_layer(dx):
        return lax.rem(x + dx + 4, 4)

    def device(dx=0, dy=0, dzh=0, dzl=0, dc=0):
        return (
            lax.rem(zh + dzh, 2) * 4 + lax.rem(y + dy + 4, 4),
            lax.rem(zl + dzl, 2) * 2 + lax.rem(c + dc, 2),
            at_layer(dx),
        )

    get_b = pltpu.make_async_copy(b_hbm.at[0], b_in, local_sem.at[0])
    get_a = pltpu.make_async_copy(a_hbm, a_in, local_sem.at[1])
    get_b.start()
    get_a.start()
    neighbours = [
        dict(dx=1), dict(dx=-1), dict(dx=2), dict(dy=1), dict(dy=-1), dict(dzl=1), dict(dzh=1), dict(dzh=1, dzl=1), dict(dc=1)
    ]
    barrier = pltpu.get_barrier_semaphore()
    for n in neighbours:
        pl.semaphore_signal(barrier, inc=1, device_id=device(**n), device_id_type=MESH)

    numbers, places, used = {}, {}, [0]
    beside = device(dx=1)
    started = {"EF": [], "E": [], "F": []}
    waited = {"E": set(), "F": set()}
    begun = set()

    def when(types, fn):
        if types == "EF":
            fn()
        else:
            pl.when(even if types == "E" else odd)(fn)

    def remote(src, dst, n, m, to):
        return pltpu.make_async_remote_copy(
            src_ref=src, dst_ref=dst, send_sem=send_sem.at[m], recv_sem=recv_sem.at[n], device_id=to, device_id_type=MESH
        )

    def put(types, key, src, dst, to):
        n = numbers.setdefault(key, len(numbers))
        m = used[0]
        used[0] += 1
        remote(src, dst, n, m, device(**to)).start()
        places[key] = dst
        started[types].append((src, dst, n, m))

    def take(key):
        if key[0] == "own":
            own_copy().wait()
            return
        n = numbers.setdefault(key, len(numbers))
        if key[0] == "a":
            dst = tiles(a_buf[key[1:4]], key[4]) if len(key) == 5 else a_buf[key[1:4]].at[pl.ds(0, CAPS)]
        elif key[0] == "m":
            dst = m_buf[key[1:4]]
        else:
            dst = places[key]
        remote(dst, dst, n, 0, beside).wait_recv()

    def piece(h, dl, dy, part=None):
        start = lax.rem(y + dy + 4, 4) * PIECE
        size = PIECE
        if part is not None:
            size = PIECE // 2
            start = start + part * size
        return b_buf.at[h, at_layer(dl), pl.ds(pl.multiple_of(start, size), size)]

    def tiles(ref, q):
        return ref.at[pl.ds(q * CUT, CUT)]

    def own_copy():
        return pltpu.make_async_copy(packed, a_buf[0, OWN, 0].at[pl.ds(0, CAPS)], local_sem.at[4])

    class Env:
        def need(self, types, *keys):
            late = {"EF": [], "E": [], "F": []}
            for key in keys:
                full = [key]
                if key[0] == "a" and (key[3] == 1 or key[4] == 0):
                    full = [("m",) + key[1:4], key]
                for name in full:
                    todo = {}
                    for t in types:
                        k = ("own",) if t == "E" and name[0] in "am" and name[1:4] == (0, OWN, 0) else name
                        if k[0] == "b" and k[2:] == (0, 0):
                            k = ("mine", k[1])
                        if k not in waited[t]:
                            waited[t].add(k)
                            todo[t] = k
                    if len(todo) == 2 and todo["E"] == todo["F"]:
                        late["EF"].append(todo["E"])
                    else:
                        for t, k in todo.items():
                            late[t].append(k)
            for t, ks in late.items():
                if ks:

                    def waits(ks=ks):
                        for k in ks:
                            if k[0] == "mine":
                                mine(k[1]).wait()
                            else:
                                take(k)

                    when(t, waits)

        def send(self, types, key, to, refs):
            def go():
                for name, src, dst in refs():
                    put(types, name or key, src, dst, to)

            when(types, go)

        def compute(self, what, *args):
            dict(unpack=unpack, multiply=multiply, code=code)[what](*args)

        def spread(self, h, d):
            return [(None, kept.at[at_layer(d), h], b_buf.at[h, x, pl.ds(pl.multiple_of(y * PIECE, PIECE), PIECE)])]

        def across(self, h, dl):
            return [(None, kept.at[x, h] if dl == 0 else piece(h, dl, 0), piece(h, dl, 0))]

        def onward(self, h, dl, dy, part):
            return [(None, piece(h, dl, dy, part), piece(h, dl, dy, part))]

        def start(self, s, q):
            slow = [(("m", 0, s, 0), slots, m_buf[0, s, 0])] if q == 0 else []
            return slow + [(None, tiles(packed, q), tiles(a_buf[0, s, 0], q))]

        def block(self, dx, s, q, to):
            slow = [(("m", to, s, 0), m_buf[dx, s, 0], m_buf[to, s, 0])] if q == 0 else []
            return slow + [(None, tiles(a_buf[dx, s, 0], q), tiles(a_buf[to, s, 0], q))]

        def twin(self, dx, s):
            here, there = pl.ds(0, CAPS), (dx, s, 1)
            return [
                (("m", dx, s, 1), m_buf[dx, s, 0], m_buf[there]),
                (None, a_buf[dx, s, 0].at[here], a_buf[there].at[here]),
            ]

        def steps(self, h):
            return [(None, steps.at[h], steps_in.at[:, pl.ds(h * SIDE, SIDE)])]

        def part(self, h, q):
            rows = pl.ds(q * PART, PART)
            return [(None, coded.at[h, rows], coded_in.at[rows, pl.ds(h * SIDE, SIDE)])]

    def mine(h):
        return pltpu.make_async_copy(kept.at[x, h], piece(h, 0, 0), local_sem.at[2 + h])

    def unpack(dx, s):
        for dc in range(2):
            key = (dx, s, dc)
            group = lax.rem(c + dc, 2)

            def tile_row(i, carry, key=key, group=group):
                at = pl.ds(pl.multiple_of(i * TILE, TILE), TILE)
                for j in range(GROUPT):
                    slot = m_buf[key][i * GROUPT + j]
                    across = pl.ds(pl.multiple_of(group * GROUP + j * TILE, TILE), TILE)
                    dense[s, dx, at, across] = a_buf[key][slot]
                return carry

            lax.fori_loop(0, ROWT, tile_row, 0, unroll=True)

    def multiply(s, dl, h):
        into = partial.at[h] if s == OTHER else out.at[:, pl.ds(h * SIDE, SIDE)]
        for m in range(4):
            at = pl.ds(m * (ROWS // 4), ROWS // 4)
            term = jnp.dot(dense[s, dl, at], b_buf[h, at_layer(dl)], preferred_element_type=jnp.float32)
            if (s, h) in begun:
                into[at] += term
            else:
                into[at] = term
        begun.add((s, h))

    def code(h):
        for q in range(PARTS):
            part = pl.ds(q * PART, PART)
            block = partial[h, part]
            most = jnp.max(jnp.abs(block), axis=0, keepdims=True)
            some = most > SMALLEST
            steps[h, q : q + 1] = jnp.where(some, most * (1.0 / LEVELS), 0.0)
            ups = jnp.where(some, LEVELS / jnp.where(some, most, 1.0), 0.0)
            coded[h, part] = jnp.round(block * ups).astype(jnp.int32).astype(jnp.int16)

    def pack():
        def scan(i, nxt):
            t = SLOTS - 1 - i
            here = a_occ[t // GROUPT, lax.rem(t, GROUPT)] != 0
            nxt = jnp.where(here, t, nxt)
            after[t] = nxt
            return nxt

        after[SLOTS] = SLOTS - 1
        first = lax.fori_loop(0, SLOTS, scan, jnp.int32(SLOTS - 1))

        def name(t, used):
            here = a_occ[t // GROUPT, lax.rem(t, GROUPT)] != 0
            slots[t] = jnp.where(here, used, CAPS)
            return used + jnp.where(here, 1, 0)

        lax.fori_loop(0, SLOTS, name, jnp.int32(0))

        def place(s, t):
            packed[s] = a_cut[t]
            return after[t + 1]

        for t in range(SLOTS):
            i, j = divmod(t, GROUPT)
            a_cut[t] = a_in[i * TILE : (i + 1) * TILE, j * TILE : (j + 1) * TILE]

        lax.fori_loop(0, CAPS, place, first)

    for key in A_KEYS:
        a_buf[key][CAPS] = jnp.zeros((TILE, TILE), jnp.bfloat16)

    env = Env()
    get_a.wait()
    pack()
    pl.semaphore_wait(barrier, len(neighbours))
    perform(("az",), env)

    @pl.when(even)
    def _():
        own_copy().start()

        def keep_slot(t, carry):
            m_buf[0, OWN, 0][t] = slots[t]
            return carry

        lax.fori_loop(0, SLOTS, keep_slot, 0)

    get_b.wait()
    for part in range(NX):
        for i in range(BROWT):
            for k in range(COLT // NX):
                j = part * (COLT // NX) + k
                h, at = divmod(k, COLT // NX // SIDES)
                tile = b_in[i * TILE : (i + 1) * TILE, j * TILE : (j + 1) * TILE]
                present = b_occ[i, 0, j] != 0
                kept[part, h, i * TILE : (i + 1) * TILE, at * TILE : (at + 1) * TILE] = jnp.where(
                    present, tile, jnp.zeros_like(tile)
                )
    for h in range(SIDES):
        mine(h).start()

    for op in PLAN:
        perform(op, env)

    for types, copies in started.items():

        def sent(copies=copies):
            for src, dst, n, m in copies:
                remote(src, dst, n, m, beside).wait_send()

        when(types, sent)


def shards(a_tiles, a_occ, b_tiles, b_occ):
    anywhere = pl.BlockSpec(memory_space=pl.ANY)
    smem = pl.BlockSpec(memory_space=pltpu.SMEM)
    own, coded, steps = pl.pallas_call(
        product_kernel,
        out_shape=(
            jax.ShapeDtypeStruct((ROWS, NCOLS), jnp.float32),
            jax.ShapeDtypeStruct((ROWS, NCOLS), jnp.int16),
            jax.ShapeDtypeStruct((PARTS, NCOLS), jnp.float32),
        ),
        in_specs=[smem, smem, anywhere, anywhere],
        out_specs=(pl.BlockSpec(memory_space=pltpu.VMEM), anywhere, anywhere),
        scratch_shapes=[pltpu.VMEM((CAPS + 1, TILE, TILE), jnp.bfloat16)] * 16
        + [pltpu.SMEM((128,), jnp.int32)] * 16
        + [
            pltpu.VMEM((ROWS, GROUP), jnp.bfloat16),
            pltpu.VMEM((SLOTS, TILE, TILE), jnp.bfloat16),
            pltpu.VMEM((PIECE, NX * NCOLS), jnp.bfloat16),
            pltpu.VMEM((CAPS, TILE, TILE), jnp.bfloat16),
            pltpu.SMEM((128,), jnp.int32),
            pltpu.SMEM((128,), jnp.int32),
            pltpu.VMEM((NX, SIDES, PIECE, SIDE), jnp.bfloat16),
            pltpu.VMEM((SIDES, NX, NY * PIECE, SIDE), jnp.bfloat16),
            pltpu.VMEM((2, NX, ROWS, 2 * GROUP), jnp.bfloat16),
            pltpu.VMEM((SIDES, ROWS, SIDE), jnp.float32),
            pltpu.VMEM((SIDES, ROWS, SIDE), jnp.int16),
            pltpu.VMEM((SIDES, PARTS, SIDE), jnp.float32),
            pltpu.SemaphoreType.DMA((200,)),
            pltpu.SemaphoreType.DMA((200,)),
            pltpu.SemaphoreType.DMA((5,)),
        ],
        compiler_params=pltpu.CompilerParams(
            collective_id=0, has_side_effects=True, vmem_limit_bytes=60 * MIB
        ),
        name="product",
    )(a_occ, b_occ.transpose(1, 0, 2), a_tiles, b_tiles)
    cut = (PARTS, PART, NCOLS)
    other = coded.reshape(cut).astype(jnp.float32) * steps[:, None, :]
    return (own.reshape(cut) + other).reshape(ROWS, NCOLS)


def solution(mesh):
    placed = (
        P("row", ("col", "layer")),
        P("row", ("col", "layer")),
        P("layer", "row", "col"),
        P("layer", "row", "col"),
    )
    return jax.shard_map(
        shards, mesh=mesh, in_specs=placed, out_specs=P("row", ("col", "layer")), check_vma=False
    )
```

```python
import jax
import jax.numpy as jnp
from jax import lax
from jax.experimental import pallas as pl
from jax.experimental.pallas import tpu as pltpu
from jax.sharding import PartitionSpec as P

MESH = pl.DeviceIdType.MESH
TILE = 128
ROWT = 8
GROUPT = 6
CAPS = 24
CUTS = 4
CUT = CAPS // CUTS
SLOTS = ROWT * GROUPT
BROWT = 3
COLT = 16
PIECE = BROWT * TILE
GROUP = GROUPT * TILE
ROWS = ROWT * TILE
NX = 4
NY = 4
NCOLS = COLT * TILE // NX
SIDES = 2
SIDE = NCOLS // SIDES
MIB = 1024 * 1024
OWN, OTHER = 0, 1
PARTS = 4
PART = ROWS // PARTS
LEVELS = 32767.0
SMALLEST = 1e-30

A_KEYS = [(dx, s, dc) for dx in range(4) for s in (OWN, OTHER) for dc in range(2)]
PLAN = [
    ("bs", 1, 2), ("by", 0, 0), ("by", 1, 0), ("bs", 0, 1), ("bs", 0, 3), ("bs", 0, 2), ("by", 1, 2), ("fq", 1),
    ("bs", 1, 3), ("by", 0, 3), ("ax", "E", 0, 1), ("ax", "F", 1, 1), ("ax", "E", 1, 1), ("ax", "F", 1, 2),
    ("fq", 0), ("bo", 1, 0), ("ac", 0, 0), ("fq", 3), ("ax", "E", 1, 0), ("by", 0, 2), ("bo", 0, 0), ("fq", 2),
    ("un", 0, 0), ("ax", "F", 1, 3), ("by", 1, 1), ("ax", "E", 1, 3), ("ax", "E", 1, 2), ("ac", 0, 1),
    ("ax", "F", 1, 0), ("by", 0, 1), ("bo", 0, 3), ("mu", 0, 0, 1), ("mu", 0, 0, 0), ("ao", "F", 1, 1), ("bs", 1, 1),
    ("un", 0, 1), ("ao", "E", 1, 3), ("ao", "F", 1, 0), ("ao", "E", 1, 0), ("ac", 3, 1), ("ao", "F", 1, 2),
    ("ax", "E", 0, 3), ("bo", 0, 2), ("un", 3, 1), ("ao", "F", 1, 3), ("av", "F", 1, 1), ("bo", 0, 1), ("bo", 1, 1),
    ("ax", "F", 0, 2), ("ac", 1, 1), ("ax", "F", 0, 0), ("ax", "E", 0, 2), ("mu", 1, 0, 0), ("un", 1, 1),
    ("av", "F", 1, 2), ("ax", "E", 0, 0), ("ax", "F", 0, 1), ("by", 1, 3), ("mu", 1, 1, 0), ("bo", 1, 2),
    ("ao", "E", 0, 1), ("ac", 2, 1), ("mu", 1, 3, 0), ("un", 2, 1), ("mu", 1, 2, 0), ("cs", 0), ("bo", 1, 3),
    ("mu", 1, 1, 1), ("ax", "F", 0, 3), ("mu", 1, 2, 1), ("ao", "F", 0, 2), ("ao", "E", 0, 3), ("ao", "F", 0, 1),
    ("mu", 1, 0, 1), ("mu", 1, 3, 1), ("ac", 1, 0), ("ao", "F", 0, 3), ("ac", 3, 0), ("ao", "F", 0, 0),
    ("ao", "E", 0, 0), ("ao", "E", 0, 2), ("cs", 1), ("un", 1, 0), ("un", 3, 0), ("mu", 0, 1, 1), ("mu", 0, 3, 0),
    ("mu", 0, 3, 1), ("cr", 0), ("ac", 2, 0), ("mu", 0, 1, 0), ("un", 2, 0), ("mu", 0, 2, 1), ("mu", 0, 2, 0),
    ("cr", 1),
]


def perform(op, env):
    kind = op[0]
    if kind == "bs":
        h, d = op[1:]
        env.send("EF", ("b", h, -d % 4, 0), dict(dx=d), lambda: env.spread(h, d))
    elif kind == "by":
        h, dl = op[1:]
        if dl:
            env.need("EF", ("b", h, dl, 0))
        for d in (1, -1):
            env.send("EF", ("b", h, dl, -d % 4), dict(dy=d), lambda: env.across(h, dl))
    elif kind == "bo":
        h, dl = op[1:]
        env.need("EF", ("b", h, dl, 3))
        env.send("EF", ("b", h, dl, 2, 0), dict(dy=1), lambda: env.onward(h, dl, -1, 0))
        env.need("EF", ("b", h, dl, 1))
        env.send("EF", ("b", h, dl, 2, 1), dict(dy=-1), lambda: env.onward(h, dl, 1, 1))
    elif kind == "az":
        for q in range(CUTS):
            env.send("E", ("a", 0, OWN, 0, q), dict(dzl=1), lambda q=q: env.start(OWN, q))
        for q in range(CUTS):
            env.send("F", ("a", 0, OTHER, 0, q), dict(dzh=1, dzl=1), lambda q=q: env.start(OTHER, q))
    elif kind == "fq":
        q = op[1]
        env.need("F", ("a", 0, OTHER, 0, q))
        env.send("F", ("a", 0, OTHER, 0, q), dict(dzl=1), lambda: env.block(0, OTHER, q, 0))
    elif kind == "ax":
        types, s, q = op[1:]
        env.need(types, ("a", 0, s, 0, q))
        for d in (1, -1):
            env.send(types, ("a", -d % 4, s, 0, q), dict(dx=d), lambda d=d: env.block(0, s, q, -d % 4))
    elif kind == "ao":
        types, s, q = op[1:]
        dx, d = (3, 1) if q < CUTS // 2 else (1, -1)
        env.need(types, ("a", dx, s, 0, q))
        env.send(types, ("a", 2, s, 0, q), dict(dx=d), lambda: env.block(dx, s, q, 2))
    elif kind == "av":
        types, s, q = op[1:]
        env.need(types, ("a", 2, s, 0, q))
        env.send(types, ("a", 2, s, 0, q), dict(dzl=1), lambda: env.block(2, s, q, 2))
    elif kind == "ac":
        dx, s = op[1:]
        for q in range(CUTS):
            env.need("EF", ("a", dx, s, 0, q))
        env.send("EF", ("a", dx, s, 1), dict(dc=1), lambda: env.twin(dx, s))
    elif kind == "un":
        dx, s = op[1:]
        for q in range(CUTS):
            env.need("EF", ("a", dx, s, 0, q))
        env.need("EF", ("a", dx, s, 1))
        env.compute("unpack", dx, s)
    elif kind == "mu":
        s, dl, h = op[1:]
        env.need("EF", ("b", h, dl, 0))
        env.need("EF", ("b", h, dl, 1), ("b", h, dl, 3), ("b", h, dl, 2, 0), ("b", h, dl, 2, 1))
        env.compute("multiply", s, dl, h)
    elif kind == "cs":
        h = op[1]
        env.compute("code", h)
        env.send("EF", ("s", h), dict(dzh=1), lambda: env.steps(h))
        for q in range(PARTS):
            env.send("EF", ("c", h, q), dict(dzh=1), lambda q=q: env.part(h, q))
    elif kind == "cr":
        h = op[1]
        env.need("EF", ("s", h))
        for q in range(PARTS):
            env.need("EF", ("c", h, q))


def product_kernel(a_occ, b_occ, a_hbm, b_hbm, out, coded_in, steps_in, *scratch):
    a_buf = dict(zip(A_KEYS, scratch[:16]))
    m_buf = dict(zip(A_KEYS, scratch[16:32]))
    (a_in, a_cut, b_in, packed, slots, after, kept, b_buf, dense, partial, coded, steps, send_sem, recv_sem, local_sem) = scratch[32:]
    row, col, x = lax.axis_index("row"), lax.axis_index("col"), lax.axis_index("layer")
    zh, y, zl, c = row // 4, lax.rem(row, 4), col // 2, lax.rem(col, 2)
    even = zh == zl
    odd = jnp.logical_not(even)

    def at_layer(dx):
        return lax.rem(x + dx + 4, 4)

    def device(dx=0, dy=0, dzh=0, dzl=0, dc=0):
        return (
            lax.rem(zh + dzh, 2) * 4 + lax.rem(y + dy + 4, 4),
            lax.rem(zl + dzl, 2) * 2 + lax.rem(c + dc, 2),
            at_layer(dx),
        )

    get_b = pltpu.make_async_copy(b_hbm.at[0], b_in, local_sem.at[0])
    get_a = pltpu.make_async_copy(a_hbm, a_in, local_sem.at[1])
    get_b.start()
    get_a.start()
    neighbours = [
        dict(dx=1), dict(dx=-1), dict(dx=2), dict(dy=1), dict(dy=-1), dict(dzl=1), dict(dzh=1), dict(dzh=1, dzl=1), dict(dc=1)
    ]
    barrier = pltpu.get_barrier_semaphore()
    for n in neighbours:
        pl.semaphore_signal(barrier, inc=1, device_id=device(**n), device_id_type=MESH)

    numbers, places, used = {}, {}, [0]
    beside = device(dx=1)
    started = {"EF": [], "E": [], "F": []}
    waited = {"E": set(), "F": set()}
    begun = set()

    def when(types, fn):
        if types == "EF":
            fn()
        else:
            pl.when(even if types == "E" else odd)(fn)

    def remote(src, dst, n, m, to):
        return pltpu.make_async_remote_copy(
            src_ref=src, dst_ref=dst, send_sem=send_sem.at[m], recv_sem=recv_sem.at[n], device_id=to, device_id_type=MESH
        )

    def put(types, key, src, dst, to):
        n = numbers.setdefault(key, len(numbers))
        m = used[0]
        used[0] += 1
        remote(src, dst, n, m, device(**to)).start()
        places[key] = dst
        started[types].append((src, dst, n, m))

    def take(key):
        if key[0] == "own":
            own_copy().wait()
            return
        n = numbers.setdefault(key, len(numbers))
        if key[0] == "a":
            dst = tiles(a_buf[key[1:4]], key[4]) if len(key) == 5 else a_buf[key[1:4]].at[pl.ds(0, CAPS)]
        elif key[0] == "m":
            dst = m_buf[key[1:4]]
        else:
            dst = places[key]
        remote(dst, dst, n, 0, beside).wait_recv()

    def piece(h, dl, dy, part=None):
        start = lax.rem(y + dy + 4, 4) * PIECE
        size = PIECE
        if part is not None:
            size = PIECE // 2
            start = start + part * size
        return b_buf.at[h, at_layer(dl), pl.ds(pl.multiple_of(start, size), size)]

    def tiles(ref, q):
        return ref.at[pl.ds(q * CUT, CUT)]

    def own_copy():
        return pltpu.make_async_copy(packed, a_buf[0, OWN, 0].at[pl.ds(0, CAPS)], local_sem.at[4])

    class Env:
        def need(self, types, *keys):
            late = {"EF": [], "E": [], "F": []}
            for key in keys:
                full = [key]
                if key[0] == "a" and (key[3] == 1 or key[4] == 0):
                    full = [("m",) + key[1:4], key]
                for name in full:
                    todo = {}
                    for t in types:
                        k = ("own",) if t == "E" and name[0] in "am" and name[1:4] == (0, OWN, 0) else name
                        if k[0] == "b" and k[2:] == (0, 0):
                            k = ("mine", k[1])
                        if k not in waited[t]:
                            waited[t].add(k)
                            todo[t] = k
                    if len(todo) == 2 and todo["E"] == todo["F"]:
                        late["EF"].append(todo["E"])
                    else:
                        for t, k in todo.items():
                            late[t].append(k)
            for t, ks in late.items():
                if ks:

                    def waits(ks=ks):
                        for k in ks:
                            if k[0] == "mine":
                                mine(k[1]).wait()
                            else:
                                take(k)

                    when(t, waits)

        def send(self, types, key, to, refs):
            def go():
                for name, src, dst in refs():
                    put(types, name or key, src, dst, to)

            when(types, go)

        def compute(self, what, *args):
            dict(unpack=unpack, multiply=multiply, code=code)[what](*args)

        def spread(self, h, d):
            return [(None, kept.at[at_layer(d), h], b_buf.at[h, x, pl.ds(pl.multiple_of(y * PIECE, PIECE), PIECE)])]

        def across(self, h, dl):
            return [(None, kept.at[x, h] if dl == 0 else piece(h, dl, 0), piece(h, dl, 0))]

        def onward(self, h, dl, dy, part):
            return [(None, piece(h, dl, dy, part), piece(h, dl, dy, part))]

        def start(self, s, q):
            slow = [(("m", 0, s, 0), slots, m_buf[0, s, 0])] if q == 0 else []
            return slow + [(None, tiles(packed, q), tiles(a_buf[0, s, 0], q))]

        def block(self, dx, s, q, to):
            slow = [(("m", to, s, 0), m_buf[dx, s, 0], m_buf[to, s, 0])] if q == 0 else []
            return slow + [(None, tiles(a_buf[dx, s, 0], q), tiles(a_buf[to, s, 0], q))]

        def twin(self, dx, s):
            here, there = pl.ds(0, CAPS), (dx, s, 1)
            return [
                (("m", dx, s, 1), m_buf[dx, s, 0], m_buf[there]),
                (None, a_buf[dx, s, 0].at[here], a_buf[there].at[here]),
            ]

        def steps(self, h):
            return [(None, steps.at[h], steps_in.at[:, pl.ds(h * SIDE, SIDE)])]

        def part(self, h, q):
            rows = pl.ds(q * PART, PART)
            return [(None, coded.at[h, rows], coded_in.at[rows, pl.ds(h * SIDE, SIDE)])]

    def mine(h):
        return pltpu.make_async_copy(kept.at[x, h], piece(h, 0, 0), local_sem.at[2 + h])

    def unpack(dx, s):
        for dc in range(2):
            key = (dx, s, dc)
            group = lax.rem(c + dc, 2)

            def tile_row(i, carry, key=key, group=group):
                at = pl.ds(pl.multiple_of(i * TILE, TILE), TILE)
                for j in range(GROUPT):
                    slot = m_buf[key][i * GROUPT + j]
                    across = pl.ds(pl.multiple_of(group * GROUP + j * TILE, TILE), TILE)
                    dense[s, dx, at, across] = a_buf[key][slot]
                return carry

            lax.fori_loop(0, ROWT, tile_row, 0, unroll=True)

    def multiply(s, dl, h):
        into = partial.at[h] if s == OTHER else out.at[:, pl.ds(h * SIDE, SIDE)]
        for m in range(4):
            at = pl.ds(m * (ROWS // 4), ROWS // 4)
            term = jnp.dot(dense[s, dl, at], b_buf[h, at_layer(dl)], preferred_element_type=jnp.float32)
            if (s, h) in begun:
                into[at] += term
            else:
                into[at] = term
        begun.add((s, h))

    def code(h):
        for q in range(PARTS):
            part = pl.ds(q * PART, PART)
            block = partial[h, part]
            most = jnp.max(jnp.abs(block), axis=0, keepdims=True)
            some = most > SMALLEST
            steps[h, q : q + 1] = jnp.where(some, most * (1.0 / LEVELS), 0.0)
            ups = jnp.where(some, LEVELS / jnp.where(some, most, 1.0), 0.0)
            coded[h, part] = jnp.round(block * ups).astype(jnp.int32).astype(jnp.int16)

    def pack():
        def scan(i, nxt):
            t = SLOTS - 1 - i
            here = a_occ[t // GROUPT, lax.rem(t, GROUPT)] != 0
            nxt = jnp.where(here, t, nxt)
            after[t] = nxt
            return nxt

        after[SLOTS] = SLOTS - 1
        first = lax.fori_loop(0, SLOTS, scan, jnp.int32(SLOTS - 1))

        def name(t, used):
            here = a_occ[t // GROUPT, lax.rem(t, GROUPT)] != 0
            slots[t] = jnp.where(here, used, CAPS)
            return used + jnp.where(here, 1, 0)

        lax.fori_loop(0, SLOTS, name, jnp.int32(0))

        def place(s, t):
            packed[s] = a_cut[t]
            return after[t + 1]

        for t in range(SLOTS):
            i, j = divmod(t, GROUPT)
            a_cut[t] = a_in[i * TILE : (i + 1) * TILE, j * TILE : (j + 1) * TILE]

        lax.fori_loop(0, CAPS, place, first)

    for key in A_KEYS:
        a_buf[key][CAPS] = jnp.zeros((TILE, TILE), jnp.bfloat16)

    env = Env()
    get_a.wait()
    pack()
    get_b.wait()
    for part in range(NX):
        for i in range(BROWT):
            for k in range(COLT // NX):
                j = part * (COLT // NX) + k
                h, at = divmod(k, COLT // NX // SIDES)
                tile = b_in[i * TILE : (i + 1) * TILE, j * TILE : (j + 1) * TILE]
                present = b_occ[i, 0, j] != 0
                kept[part, h, i * TILE : (i + 1) * TILE, at * TILE : (at + 1) * TILE] = jnp.where(
                    present, tile, jnp.zeros_like(tile)
                )
    for h in range(SIDES):
        mine(h).start()
    pl.semaphore_wait(barrier, len(neighbours))
    perform(("az",), env)

    @pl.when(even)
    def _():
        own_copy().start()

        def keep_slot(t, carry):
            m_buf[0, OWN, 0][t] = slots[t]
            return carry

        lax.fori_loop(0, SLOTS, keep_slot, 0)


    for op in PLAN:
        perform(op, env)

    for types, copies in started.items():

        def sent(copies=copies):
            for src, dst, n, m in copies:
                remote(src, dst, n, m, beside).wait_send()

        when(types, sent)


def shards(a_tiles, a_occ, b_tiles, b_occ):
    anywhere = pl.BlockSpec(memory_space=pl.ANY)
    smem = pl.BlockSpec(memory_space=pltpu.SMEM)
    own, coded, steps = pl.pallas_call(
        product_kernel,
        out_shape=(
            jax.ShapeDtypeStruct((ROWS, NCOLS), jnp.float32),
            jax.ShapeDtypeStruct((ROWS, NCOLS), jnp.int16),
            jax.ShapeDtypeStruct((PARTS, NCOLS), jnp.float32),
        ),
        in_specs=[smem, smem, anywhere, anywhere],
        out_specs=(pl.BlockSpec(memory_space=pltpu.VMEM), anywhere, anywhere),
        scratch_shapes=[pltpu.VMEM((CAPS + 1, TILE, TILE), jnp.bfloat16)] * 16
        + [pltpu.SMEM((128,), jnp.int32)] * 16
        + [
            pltpu.VMEM((ROWS, GROUP), jnp.bfloat16),
            pltpu.VMEM((SLOTS, TILE, TILE), jnp.bfloat16),
            pltpu.VMEM((PIECE, NX * NCOLS), jnp.bfloat16),
            pltpu.VMEM((CAPS, TILE, TILE), jnp.bfloat16),
            pltpu.SMEM((128,), jnp.int32),
            pltpu.SMEM((128,), jnp.int32),
            pltpu.VMEM((NX, SIDES, PIECE, SIDE), jnp.bfloat16),
            pltpu.VMEM((SIDES, NX, NY * PIECE, SIDE), jnp.bfloat16),
            pltpu.VMEM((2, NX, ROWS, 2 * GROUP), jnp.bfloat16),
            pltpu.VMEM((SIDES, ROWS, SIDE), jnp.float32),
            pltpu.VMEM((SIDES, ROWS, SIDE), jnp.int16),
            pltpu.VMEM((SIDES, PARTS, SIDE), jnp.float32),
            pltpu.SemaphoreType.DMA((200,)),
            pltpu.SemaphoreType.DMA((200,)),
            pltpu.SemaphoreType.DMA((5,)),
        ],
        compiler_params=pltpu.CompilerParams(
            collective_id=0, has_side_effects=True, vmem_limit_bytes=60 * MIB
        ),
        name="product",
    )(a_occ, b_occ.transpose(1, 0, 2), a_tiles, b_tiles)
    cut = (PARTS, PART, NCOLS)
    other = coded.reshape(cut).astype(jnp.float32) * steps[:, None, :]
    return (own.reshape(cut) + other).reshape(ROWS, NCOLS)


def solution(mesh):
    placed = (
        P("row", ("col", "layer")),
        P("row", ("col", "layer")),
        P("layer", "row", "col"),
        P("layer", "row", "col"),
    )
    return jax.shard_map(
        shards, mesh=mesh, in_specs=placed, out_specs=P("row", ("col", "layer")), check_vma=False
    )
```
